256 devices in a mesh: frame: 32 (over y_hi, z, core), patch: 8 (over y_lo, x).
Axes of the slice: x: 4, y: 4 (y_hi: 2, y_lo: 2; y = y_hi * 2 + y_lo), z: 8, core: 2. Of those that a mesh axis runs over, the one named last changes fastest.
Arguments:
- video: bfloat16 [256, 256, 1024], P('frame', 'patch'), may hold values from -6 to 6
- gain_space: float32 [1024], replicated, may hold values from 0.25 to 1.75
- qkv_space: bfloat16 [3, 1024, 1024], P(None, None, 'patch'), may hold values from -0.1875 to 0.1875
- out_space: bfloat16 [1024, 1024], P('patch'), may hold values from -2 to 2
- gain_time: float32 [1024], replicated, may hold values from 0.25 to 1.75
- qkv_time: bfloat16 [3, 1024, 1024], P(None, None, 'patch'), may hold values from -0.1875 to 0.1875
- out_time: bfloat16 [1024, 1024], P('patch'), may hold values from -0.1875 to 0.1875
- gain_mlp: float32 [1024], replicated, may hold values from 0.25 to 1.75
- w_in: bfloat16 [1024, 4096], P(None, 'patch'), may hold values from -0.1875 to 0.1875
- w_out: bfloat16 [4096, 1024], P('patch'), may hold values from -0.09375 to 0.09375
- score_head: float32 [1024], replicated, may hold values from -0.1875 to 0.1875
Outputs:
- features: bfloat16 [256, 256, 1024], P('frame', 'patch')
- score: float32 [2], replicated
The draws below stay inside these ranges and needn't reach their ends.
All inputs are finite; a program needn't handle non-finite values.
Results may differ from the reference program's by a relative error of at most 0.02.
Values may be sent and summed in bfloat16 or wider, within the bound.
No kernel may reach another device: no remote copies, remote signals or barrier semaphores. Data moves between devices by JAX's collectives and lax.ppermute only.
A program may use at most 64 MiB of HBM per device.

```python
import jax
import jax.numpy as jnp
from jax import lax

D = 1024
HEADS = 16
HDIM = 64
FF = 4096
CLIPS = 2
ROWS = 256
PATCHES = 256
CLIP_FRAMES = 128
N_PATCH = 8


def levels(own_key, extent, pieces, least, largest):
    gain, own = 1.0, jax.random.fold_in(own_key, 6)
    for axis_at, blocks in pieces:
        steps = jnp.exp(jax.random.uniform(jax.random.fold_in(own, axis_at), (blocks,), jnp.float32, least / len(pieces), largest / len(pieces)))
        gain = gain * jnp.repeat(steps, extent[axis_at] // blocks).reshape([-1 if axis == axis_at else 1 for axis in range(len(extent))])
    return gain


def centred(rng, shape, deviation, most, shards=(), kind=jnp.bfloat16):
    gain = levels(rng, shape, shards, -0.22, 0.18) if shards else 1.0
    result = jax.random.normal(rng, shape, jnp.float32) * deviation * gain
    return jnp.minimum(jnp.maximum(result, -most), most).astype(kind)


def setup_inputs(seed: int = 0) -> dict:
    keys = jax.random.split(jax.random.key(seed), 12)
    video = centred(keys[0], (ROWS, PATCHES, D), 1.0, 6.0, ((0, 32), (1, 8)))
    gain_space = jnp.clip(1.0 + 0.15 * jax.random.normal(keys[1], (D,), jnp.float32), 0.25, 1.75)
    qkv_space = centred(keys[2], (3, D, D), D ** -0.5, 0.1875, ((2, 8),))
    out_space = centred(keys[3], (D, D), 0.15, 2.0, ((0, 8),))
    gain_time = jnp.clip(1.0 + 0.15 * jax.random.normal(keys[4], (D,), jnp.float32), 0.25, 1.75)
    qkv_time = centred(keys[5], (3, D, D), D ** -0.5, 0.1875, ((2, 8),))
    out_time = centred(keys[6], (D, D), D ** -0.5, 0.1875, ((0, 8),))
    gain_mlp = jnp.clip(1.0 + 0.15 * jax.random.normal(keys[7], (D,), jnp.float32), 0.25, 1.75)
    w_in = centred(keys[8], (D, FF), D ** -0.5, 0.1875, ((1, 8),))
    w_out = centred(keys[9], (FF, D), FF ** -0.5, 0.09375, ((0, 8),))
    score_head = centred(keys[10], (D,), D ** -0.5, 0.1875, (), jnp.float32)
    return {"video": video, "gain_space": gain_space, "qkv_space": qkv_space, "out_space": out_space, "gain_time": gain_time, "qkv_time": qkv_time, "out_time": out_time, "gain_mlp": gain_mlp, "w_in": w_in, "w_out": w_out, "score_head": score_head}


def rms_norm(values, gains):
    floats = values.astype(jnp.float32)
    scaled = floats * lax.rsqrt(lax.optimization_barrier(jnp.mean(floats * floats, axis=-1, keepdims=True)) + 1e-06)
    return (scaled * gains).astype(jnp.bfloat16)

def project(normed, weights):
    flat = normed.reshape(-1, D)
    return tuple((jnp.dot(flat, weights[member], preferred_element_type=jnp.float32).astype(jnp.bfloat16).reshape(normed.shape) for member in range(3)))

def attend(queries, keys_in, values_in):
    scores = jnp.einsum('phe,qhe->hpq', queries.astype(jnp.float32), keys_in.astype(jnp.float32)) * HDIM ** (-0.5)
    probs = jax.nn.softmax(scores, axis=-1).astype(jnp.bfloat16)
    return jnp.einsum('hpq,qhe->phe', probs.astype(jnp.float32), values_in.astype(jnp.float32)).astype(jnp.bfloat16)

def grouped_sum(residual, inputs, weights):
    width = inputs.shape[-1] // N_PATCH
    total = residual.astype(jnp.float32)
    for group in range(N_PATCH):
        columns = inputs[..., group * width:(group + 1) * width].reshape(-1, width)
        partial_value = jnp.dot(columns, weights[group * width:(group + 1) * width], preferred_element_type=jnp.float32).astype(jnp.bfloat16)
        total = total + partial_value.astype(jnp.float32).reshape(residual.shape)
    return total.astype(jnp.bfloat16)

def reference(video, gain_space, qkv_space, out_space, gain_time, qkv_time, out_time, gain_mlp, w_in, w_out, score_head):
    normed_space = rms_norm(video, gain_space)
    q_space, k_space, v_space = project(normed_space, qkv_space)

    def frame_block(items):
        shaped = [item.reshape(PATCHES, HEADS, HDIM) for item in items]
        return attend(shaped[0], shaped[1], shaped[2]).reshape(PATCHES, D)
    context_space = lax.map(frame_block, (q_space, k_space, v_space))
    after_space = grouped_sum(video, context_space, out_space)
    normed_time = rms_norm(after_space, gain_time)
    triples = project(normed_time, qkv_time)
    moved = [jnp.transpose(item.reshape(CLIPS, CLIP_FRAMES, PATCHES, HEADS, HDIM), (2, 0, 1, 3, 4)) for item in triples]

    def patch_block(items):
        return jax.vmap(attend)(items[0], items[1], items[2])
    context_moved = lax.map(patch_block, (moved[0], moved[1], moved[2]))
    context_time = jnp.transpose(context_moved, (1, 2, 0, 3, 4)).reshape(ROWS, PATCHES, D)
    after_time = grouped_sum(after_space, context_time, out_time)
    normed_mlp = rms_norm(after_time, gain_mlp)
    hidden = jax.nn.gelu(jnp.dot(normed_mlp.reshape(-1, D), w_in, preferred_element_type=jnp.float32), approximate=False).astype(jnp.bfloat16)
    features = grouped_sum(after_time, hidden.reshape(ROWS, PATCHES, FF), w_out)
    token_score = lax.optimization_barrier(jnp.sum(features.astype(jnp.float32) * score_head, axis=-1))
    per_clip = lax.optimization_barrier(jnp.sum(jnp.exp(token_score).reshape(CLIPS, CLIP_FRAMES * PATCHES), axis=1))
    score = jnp.log(per_clip / (CLIP_FRAMES * PATCHES))
    return (features, score)
```

```python
import functools

import jax
import jax.numpy as jnp
from jax import lax
from jax.experimental import pallas as pl
from jax.experimental.pallas import tpu as pltpu
from jax.sharding import PartitionSpec as P

HDIM = 64
CLIPS = 2
NX, NY, NZ, NCORE = 4, 4, 8, 2
AXES = ("frame", "patch")
BF16 = jnp.bfloat16
F32 = jnp.float32


def place(flat):
    frame, patch = divmod(flat, NX * 2)
    y_hi, rest = divmod(frame, NZ * NCORE)
    z, core = divmod(rest, NCORE)
    y_lo, x = divmod(patch, NX)
    return x, y_hi * 2 + y_lo, z, core


def flat_of(x, y, z, core):
    y_hi, y_lo = divmod(y % NY, 2)
    return ((y_hi * NZ + z % NZ) * NCORE + core % NCORE) * (NX * 2) + y_lo * NX + x % NX


def shift(value, dx=0, dy=0, dz=0, dc=0):
    pairs = []
    for flat in range(NX * NY * NZ * NCORE):
        x, y, z, core = place(flat)
        pairs.append((flat, flat_of(x + dx, y + dy, z + dz, core + dc)))
    return lax.ppermute(value, AXES, pairs)


def dot(left, right):
    return jnp.dot(left, right, preferred_element_type=F32)


def gather_half(own):
    rows = own.shape[0]
    cut = rows // 2
    from_left = shift(own, dx=1)
    from_right = shift(own, dx=-1)
    other_lo = shift(own[:cut], dy=1)
    other_hi = shift(own[cut:], dy=-1)
    far_lo = shift(from_left[:cut], dx=1)
    far_hi = shift(from_right[cut:], dx=-1)
    other_left = shift(from_left, dy=1)
    other_right = shift(from_right, dy=-1)
    other_far_lo = shift(far_lo, dy=1)
    other_far_hi = shift(far_hi, dy=-1)
    parts = [
        own,
        other_lo,
        other_hi,
        from_left,
        from_right,
        other_left,
        other_right,
        far_lo,
        far_hi,
        other_far_lo,
        other_far_hi,
    ]
    mine = jnp.concatenate(parts, axis=0).reshape((8,) + own.shape)
    theirs = shift(mine, dc=1)
    return mine, theirs


def attention_kernel(
    core_ref, x_ref, gain_ref, mine_ref, theirs_ref, o_ref, normed_ref, total_ref, *, interleaved
):
    step = pl.program_id(0)
    core = core_ref[0]
    half = x_ref.shape[1] // 2
    at_mine = pl.multiple_of(core * half, half)
    at_theirs = pl.multiple_of(half - core * half, half)

    @pl.when(step == 0)
    def _():
        values = x_ref[...].astype(F32)
        scale = lax.rsqrt(jnp.mean(values * values, axis=-1, keepdims=True) + 1e-06)
        normed_ref[...] = (values * scale * gain_ref[...]).astype(BF16)
        total_ref[...] = values

    x_mine = normed_ref[:, pl.ds(at_mine, half)]
    x_theirs = normed_ref[:, pl.ds(at_theirs, half)]

    def project(member):
        w_mine = jnp.concatenate([mine_ref[0, member], mine_ref[1, member]], axis=1)
        w_theirs = jnp.concatenate([theirs_ref[0, member], theirs_ref[1, member]], axis=1)
        return dot(x_mine, w_mine) + dot(x_theirs, w_theirs)

    queries = (project(0) * HDIM ** (-0.5)).astype(BF16)
    keys = project(1).astype(BF16)
    values_in = project(2).astype(BF16)
    tokens = queries.shape[0]
    lane = lax.broadcasted_iota(jnp.int32, (tokens, 2 * HDIM), 1)
    if interleaved:
        row = lax.broadcasted_iota(jnp.int32, (tokens, tokens), 0)
        col = lax.broadcasted_iota(jnp.int32, (tokens, tokens), 1)
        same = (row & 1) == (col & 1)
    contexts = []
    for pair in range(2):
        cols = slice(pair * 2 * HDIM, (pair + 1) * 2 * HDIM)
        q_pair, k_pair, v_pair = queries[:, cols], keys[:, cols], values_in[:, cols]
        results = []
        for head in range(2):
            q_head = jnp.where((lane < HDIM) == (head == 0), q_pair, jnp.zeros_like(q_pair))
            scores = lax.dot_general(
                q_head, k_pair, (((1,), (1,)), ((), ())), preferred_element_type=F32
            )
            if interleaved:
                scores = jnp.where(same, scores, -jnp.inf)
            top = jnp.max(scores, axis=-1, keepdims=True)
            weights = jnp.exp(scores - top)
            denom = jnp.sum(weights, axis=-1, keepdims=True)
            results.append(dot(weights.astype(BF16), v_pair) / denom)
        contexts.append(jnp.where(lane < HDIM, results[0], results[1]).astype(BF16))
    context = jnp.concatenate(contexts, axis=1)
    for ref, start in ((mine_ref, at_mine), (theirs_ref, at_theirs)):
        blocks = []
        for block in range(4):
            rows = slice(block * 128, (block + 1) * 128)
            blocks.append(jnp.concatenate([ref[0, 3, rows], ref[1, 3, rows]], axis=0))
        w_out = jnp.concatenate(blocks, axis=1)
        total_ref[:, pl.ds(start, half)] += dot(context, w_out)

    @pl.when(step == pl.num_programs(0) - 1)
    def _():
        o_ref[...] = total_ref[...].astype(BF16)


def attention_block(core, tokens, gain, mine, theirs, interleaved):
    rows, width = tokens.shape
    weight_spec = pl.BlockSpec((2,) + mine.shape[1:], lambda s: (s, 0, 0, 0))
    return pl.pallas_call(
        functools.partial(attention_kernel, interleaved=interleaved),
        out_shape=jax.ShapeDtypeStruct((rows, width), BF16),
        grid=(4,),
        in_specs=[
            pl.BlockSpec(memory_space=pltpu.SMEM),
            pl.BlockSpec((rows, width), lambda s: (0, 0)),
            pl.BlockSpec((1, width), lambda s: (0, 0)),
            weight_spec,
            weight_spec,
        ],
        out_specs=pl.BlockSpec((rows, width), lambda s: (0, 0)),
        scratch_shapes=[pltpu.VMEM((rows, width), BF16), pltpu.VMEM((rows, width), F32)],
        compiler_params=pltpu.CompilerParams(vmem_limit_bytes=40 * 2**20),
        cost_estimate=pl.CostEstimate(
            flops=2 * rows * width * width * 5, bytes_accessed=10 * 2**20, transcendentals=2**20
        ),
    )(core, tokens, gain.reshape(1, width), mine, theirs)


def mlp_kernel(
    x_ref, gain_ref, head_ref, mine_ref, theirs_ref, o_ref, sum_ref, normed_ref, total_ref
):
    step = pl.program_id(0)

    @pl.when(step == 0)
    def _():
        values = x_ref[...].astype(F32)
        scale = lax.rsqrt(jnp.mean(values * values, axis=-1, keepdims=True) + 1e-06)
        normed_ref[...] = (values * scale * gain_ref[...]).astype(BF16)
        total_ref[...] = values

    units = mine_ref.shape[1] // 2
    for ref in (mine_ref, theirs_ref):
        inner = None
        for block in range(x_ref.shape[1] // units):
            cols = slice(block * units, (block + 1) * units)
            term = dot(normed_ref[:, cols], ref[0, :units, cols])
            inner = term if inner is None else inner + term
        hidden = (0.5 * inner * (1.0 + lax.erf(inner * 2.0 ** (-0.5)))).astype(BF16)
        total_ref[...] += dot(hidden, ref[0, units:])

    @pl.when(step == pl.num_programs(0) - 1)
    def _():
        features = total_ref[...].astype(BF16)
        o_ref[...] = features
        token_score = jnp.sum(features.astype(F32) * head_ref[...], axis=-1, keepdims=True)
        sum_ref[...] = jnp.zeros(sum_ref.shape, F32) + jnp.sum(jnp.exp(token_score))


def mlp_block(tokens, gain, score_head, mine, theirs):
    rows, width = tokens.shape
    weight_spec = pl.BlockSpec((1,) + mine.shape[1:], lambda s: (s, 0, 0))
    whole = pl.BlockSpec((1, width), lambda s: (0, 0))
    return pl.pallas_call(
        mlp_kernel,
        out_shape=(
            jax.ShapeDtypeStruct((rows, width), BF16),
            jax.ShapeDtypeStruct((8, 128), F32),
        ),
        grid=(8,),
        in_specs=[
            pl.BlockSpec((rows, width), lambda s: (0, 0)),
            whole,
            whole,
            weight_spec,
            weight_spec,
        ],
        out_specs=(
            pl.BlockSpec((rows, width), lambda s: (0, 0)),
            pl.BlockSpec((8, 128), lambda s: (0, 0)),
        ),
        scratch_shapes=[pltpu.VMEM((rows, width), BF16), pltpu.VMEM((rows, width), F32)],
        compiler_params=pltpu.CompilerParams(vmem_limit_bytes=40 * 2**20),
        cost_estimate=pl.CostEstimate(
            flops=2 * rows * width * width * 8, bytes_accessed=18 * 2**20, transcendentals=2**20
        ),
    )(tokens, gain.reshape(1, width), score_head.reshape(1, width), mine, theirs)


def pack_attention(qkv, out, core):
    half = qkv.shape[1] // 2
    own_qkv = lax.dynamic_slice_in_dim(qkv, core * half, half, axis=1)
    own_out = lax.dynamic_slice_in_dim(out, core * half, half, axis=1)
    local, _ = own_out.shape
    blocks = jnp.transpose(own_out.reshape(local, half // 128, 128), (1, 0, 2))
    return jnp.concatenate([own_qkv.reshape(3 * half, 128), blocks.reshape(half, 128)], axis=0)


def pack_mlp(w_in, w_out, core):
    width = w_in.shape[0]
    units = w_in.shape[1] // 2
    own_in = lax.dynamic_slice_in_dim(w_in, core * units, units, axis=1)
    own_out = lax.dynamic_slice_in_dim(w_out, core * units, units, axis=0)
    blocks = jnp.transpose(own_in.reshape(width // units, units, units), (1, 0, 2))
    return jnp.concatenate([blocks.reshape(units, width), own_out], axis=0)


def shards(
    video,
    gain_space,
    qkv_space,
    out_space,
    gain_time,
    qkv_time,
    out_time,
    gain_mlp,
    w_in,
    w_out,
    score_head,
):
    frames, local_patches, width = video.shape
    patch_count = NX * 2
    clip_ranks = NZ * NCORE
    rows = frames * local_patches
    pairs = local_patches // clip_ranks
    frame_index = lax.axis_index("frame")
    core = frame_index % NCORE
    core_scalar = core.astype(jnp.int32).reshape(1)

    space_mine, space_theirs = gather_half(pack_attention(qkv_space, out_space, core))
    time_mine, time_theirs = gather_half(pack_attention(qkv_time, out_time, core))
    mlp_mine, mlp_theirs = gather_half(pack_mlp(w_in, w_out, core))
    attention_shape = (8, 4, width // 2, 128)

    by_frame = lax.all_to_all(video, "patch", 0, 0, tiled=True)
    by_frame = jnp.transpose(
        by_frame.reshape(patch_count, clip_ranks, pairs, width), (1, 0, 2, 3)
    ).reshape(rows, width)
    after_space = attention_block(
        core_scalar,
        by_frame,
        gain_space,
        space_mine.reshape(attention_shape),
        space_theirs.reshape(attention_shape),
        False,
    )
    clip_groups = [[c * 128 + i for i in range(128)] for c in range(CLIPS)]
    by_patch = lax.all_to_all(
        after_space, AXES, 0, 0, tiled=True, axis_index_groups=clip_groups
    )
    after_time = attention_block(
        core_scalar,
        by_patch,
        gain_time,
        time_mine.reshape(attention_shape),
        time_theirs.reshape(attention_shape),
        True,
    )
    frame_groups = [[c * clip_ranks + i for i in range(clip_ranks)] for c in range(CLIPS)]
    at_home = lax.all_to_all(
        after_time, "frame", 0, 0, tiled=True, axis_index_groups=frame_groups
    )
    tokens, sums = mlp_block(at_home, gain_mlp, score_head, mlp_mine, mlp_theirs)
    features = jnp.transpose(
        tokens.reshape(clip_ranks, frames, pairs, width), (1, 0, 2, 3)
    ).reshape(frames, local_patches, width)

    for bit in range(7):
        sums = sums + lax.ppermute(sums, AXES, [(i, i ^ (1 << bit)) for i in range(256)])
    other = lax.ppermute(sums, AXES, [(i, i ^ 128) for i in range(256)])
    first = frame_index < clip_ranks
    per_clip = jnp.stack(
        [jnp.where(first, sums[0, 0], other[0, 0]), jnp.where(first, other[0, 0], sums[0, 0])]
    )
    score = jnp.log(per_clip / (frames * clip_ranks * local_patches * patch_count))
    return (features, score)


def solution(mesh):
    placed = (
        P("frame", "patch", None),
        P(),
        P(None, None, "patch"),
        P("patch", None),
        P(),
        P(None, None, "patch"),
        P("patch", None),
        P(),
        P(None, "patch"),
        P("patch", None),
        P(),
    )
    return jax.shard_map(
        shards,
        mesh=mesh,
        in_specs=placed,
        out_specs=(P("frame", "patch", None), P()),
        check_vma=False,
    )
```

```python
import functools

import jax
import jax.numpy as jnp
from jax import lax
from jax.experimental import pallas as pl
from jax.experimental.pallas import tpu as pltpu
from jax.sharding import PartitionSpec as P

HDIM = 64
CLIPS = 2
NX, NY, NZ, NCORE = 4, 4, 8, 2
AXES = ("frame", "patch")
BF16 = jnp.bfloat16
F32 = jnp.float32


def place(flat):
    frame, patch = divmod(flat, NX * 2)
    y_hi, rest = divmod(frame, NZ * NCORE)
    z, core = divmod(rest, NCORE)
    y_lo, x = divmod(patch, NX)
    return x, y_hi * 2 + y_lo, z, core


def flat_of(x, y, z, core):
    y_hi, y_lo = divmod(y % NY, 2)
    return ((y_hi * NZ + z % NZ) * NCORE + core % NCORE) * (NX * 2) + y_lo * NX + x % NX


def shift(value, dx=0, dy=0, dz=0, dc=0):
    pairs = []
    for flat in range(NX * NY * NZ * NCORE):
        x, y, z, core = place(flat)
        pairs.append((flat, flat_of(x + dx, y + dy, z + dz, core + dc)))
    return lax.ppermute(value, AXES, pairs)


def dot(left, right):
    return jnp.dot(left, right, preferred_element_type=F32)


def barrier(*values):
    return lax.optimization_barrier(values)


def first_phase_x(own):
    return shift(own, dx=1), shift(own, dx=-1)


def first_phase_y(own):
    cut = own.shape[0] // 2
    return shift(own[:cut], dy=1), shift(own[cut:], dy=-1)


def second_phase(left, right):
    cut = left.shape[0] // 2
    far_lo, far_hi = shift(left[:cut], dx=1), shift(right[cut:], dx=-1)
    return far_lo, far_hi, shift(left, dy=1), shift(right, dy=-1)


def third_phase(far_lo, far_hi):
    return shift(far_lo, dy=1), shift(far_hi, dy=-1)


def four(*parts):
    joined = jnp.concatenate(parts, axis=0)
    return joined.reshape((4, joined.shape[0] // 4) + joined.shape[1:])


def swap(part):
    return shift(part, dc=1)


def attend(queries, keys, values_in, interleaved):
    tokens = queries.shape[0]
    lane = lax.broadcasted_iota(jnp.int32, (tokens, 2 * HDIM), 1)
    if interleaved:
        row = lax.broadcasted_iota(jnp.int32, (tokens, tokens), 0)
        col = lax.broadcasted_iota(jnp.int32, (tokens, tokens), 1)
        same = (row & 1) == (col & 1)
    contexts = []
    for pair in range(2):
        cols = slice(pair * 2 * HDIM, (pair + 1) * 2 * HDIM)
        q_pair, k_pair, v_pair = queries[:, cols], keys[:, cols], values_in[:, cols]
        results = []
        for head in range(2):
            q_head = jnp.where((lane < HDIM) == (head == 0), q_pair, jnp.zeros_like(q_pair))
            scores = lax.dot_general(
                q_head, k_pair, (((1,), (1,)), ((), ())), preferred_element_type=F32
            )
            if interleaved:
                scores = jnp.where(same, scores, -jnp.inf)
            top = jnp.max(scores, axis=-1, keepdims=True)
            weights = jnp.exp(scores - top)
            denom = jnp.sum(weights, axis=-1, keepdims=True)
            results.append(dot(weights.astype(BF16), v_pair) / denom)
        contexts.append(jnp.where(lane < HDIM, results[0], results[1]).astype(BF16))
    return jnp.concatenate(contexts, axis=1)


def start_norm(x_ref, gain_ref, normed_ref, total_ref):
    values = x_ref[...].astype(F32)
    scale = lax.rsqrt(jnp.mean(values * values, axis=-1, keepdims=True) + 1e-06)
    normed_ref[...] = (values * scale * gain_ref[...]).astype(BF16)
    total_ref[...] = values


def space_kernel(
    core_ref, x_ref, gain_ref, near_ref, near_other_ref, far_ref, far_other_ref, o_ref,
    normed_ref, total_ref,
):
    step = pl.program_id(0)
    core = core_ref[0]
    half = x_ref.shape[1] // 2
    at_mine = pl.multiple_of(core * half, half)
    at_theirs = pl.multiple_of(half - core * half, half)

    @pl.when(step == 0)
    def _():
        start_norm(x_ref, gain_ref, normed_ref, total_ref)

    def heads(mine_ref, theirs_ref):
        x_mine = normed_ref[:, pl.ds(at_mine, half)]
        x_theirs = normed_ref[:, pl.ds(at_theirs, half)]

        def project(member):
            w_mine = jnp.concatenate([mine_ref[0, member], mine_ref[1, member]], axis=1)
            w_theirs = jnp.concatenate([theirs_ref[0, member], theirs_ref[1, member]], axis=1)
            return dot(x_mine, w_mine) + dot(x_theirs, w_theirs)

        queries = (project(0) * HDIM ** (-0.5)).astype(BF16)
        context = attend(queries, project(1).astype(BF16), project(2).astype(BF16), False)
        for ref, start in ((mine_ref, at_mine), (theirs_ref, at_theirs)):
            blocks = []
            for block in range(4):
                rows = slice(block * 128, (block + 1) * 128)
                blocks.append(jnp.concatenate([ref[0, 3, rows], ref[1, 3, rows]], axis=0))
            w_out = jnp.concatenate(blocks, axis=1)
            total_ref[:, pl.ds(start, half)] += dot(context, w_out)

    @pl.when(step < 2)
    def _():
        heads(near_ref, near_other_ref)

    @pl.when(step >= 2)
    def _():
        heads(far_ref, far_other_ref)

    @pl.when(step == pl.num_programs(0) - 1)
    def _():
        o_ref[...] = total_ref[...].astype(BF16)


ATTENTION_COST = pl.CostEstimate(
    flops=10 * 256 * 2**20, bytes_accessed=10 * 2**20, transcendentals=2**20
)
MLP_COST = pl.CostEstimate(
    flops=16 * 256 * 2**20, bytes_accessed=18 * 2**20, transcendentals=2**20
)
KERNEL_PARAMS = pltpu.CompilerParams(vmem_limit_bytes=40 * 2**20)


def space_block(core, tokens, gain, near, near_other, far, far_other):
    rows, width = tokens.shape
    shape = (2, 4, width // 2, 128)
    near_spec = pl.BlockSpec(shape, lambda s: (jnp.minimum(s, 1), 0, 0, 0))
    far_spec = pl.BlockSpec(shape, lambda s: (jnp.maximum(s - 2, 0), 0, 0, 0))
    whole = (4, 4, width // 2, 128)
    return pl.pallas_call(
        space_kernel,
        out_shape=jax.ShapeDtypeStruct((rows, width), BF16),
        grid=(4,),
        in_specs=[
            pl.BlockSpec(memory_space=pltpu.SMEM),
            pl.BlockSpec((rows, width), lambda s: (0, 0)),
            pl.BlockSpec((1, width), lambda s: (0, 0)),
            near_spec,
            near_spec,
            far_spec,
            far_spec,
        ],
        out_specs=pl.BlockSpec((rows, width), lambda s: (0, 0)),
        scratch_shapes=[pltpu.VMEM((rows, width), BF16), pltpu.VMEM((rows, width), F32)],
        compiler_params=KERNEL_PARAMS,
        cost_estimate=ATTENTION_COST,
    )(
        core,
        tokens,
        gain.reshape(1, width),
        near.reshape(whole),
        near_other.reshape(whole),
        far.reshape(whole),
        far_other.reshape(whole),
    )


def time_kernel(x_ref, gain_ref, weights_ref, o_ref, normed_ref, total_ref):
    step = pl.program_id(0)
    width = x_ref.shape[1]
    depth = weights_ref.shape[2] // 4

    @pl.when(step == 0)
    def _():
        start_norm(x_ref, gain_ref, normed_ref, total_ref)

    def member_of(shard, member):
        block = weights_ref[:, shard, member * depth : (member + 1) * depth, :]
        return block.reshape(width, 128)

    def project(member):
        weights = jnp.concatenate([member_of(0, member), member_of(1, member)], axis=1)
        return dot(normed_ref[...], weights)

    queries = (project(0) * HDIM ** (-0.5)).astype(BF16)
    context = attend(queries, project(1).astype(BF16), project(2).astype(BF16), True)
    outs = (member_of(0, 3), member_of(1, 3))
    blocks = []
    for block in range(width // 128):
        rows = slice(block * 128, (block + 1) * 128)
        blocks.append(jnp.concatenate([outs[0][rows], outs[1][rows]], axis=0))
    total_ref[...] += dot(context, jnp.concatenate(blocks, axis=1))

    @pl.when(step == pl.num_programs(0) - 1)
    def _():
        o_ref[...] = total_ref[...].astype(BF16)


def time_block(tokens, gain, weights):
    rows, width = tokens.shape
    ranks, shard_count, depth, lanes = weights.shape
    return pl.pallas_call(
        time_kernel,
        out_shape=jax.ShapeDtypeStruct((rows, width), BF16),
        grid=(shard_count // 2,),
        in_specs=[
            pl.BlockSpec((rows, width), lambda s: (0, 0)),
            pl.BlockSpec((1, width), lambda s: (0, 0)),
            pl.BlockSpec((ranks, 2, depth, lanes), lambda s: (0, s, 0, 0)),
        ],
        out_specs=pl.BlockSpec((rows, width), lambda s: (0, 0)),
        scratch_shapes=[pltpu.VMEM((rows, width), BF16), pltpu.VMEM((rows, width), F32)],
        compiler_params=KERNEL_PARAMS,
        cost_estimate=ATTENTION_COST,
    )(tokens, gain.reshape(1, width), weights)


def mlp_kernel(
    x_ref, gain_ref, head_ref, near_ref, near_other_ref, far_ref, far_other_ref, o_ref, sum_ref,
    normed_ref, total_ref,
):
    step = pl.program_id(0)

    @pl.when(step == 0)
    def _():
        start_norm(x_ref, gain_ref, normed_ref, total_ref)

    def units_of(*refs):
        for ref in refs:
            units = ref.shape[1] // 2
            inner = None
            for block in range(x_ref.shape[1] // units):
                cols = slice(block * units, (block + 1) * units)
                term = dot(normed_ref[:, cols], ref[0, :units, cols])
                inner = term if inner is None else inner + term
            hidden = (0.5 * inner * (1.0 + lax.erf(inner * 2.0 ** (-0.5)))).astype(BF16)
            total_ref[...] += dot(hidden, ref[0, units:])

    @pl.when(step < 4)
    def _():
        units_of(near_ref, near_other_ref)

    @pl.when(step >= 4)
    def _():
        units_of(far_ref, far_other_ref)

    @pl.when(step == pl.num_programs(0) - 1)
    def _():
        features = total_ref[...].astype(BF16)
        o_ref[...] = features
        token_score = jnp.sum(features.astype(F32) * head_ref[...], axis=-1, keepdims=True)
        sum_ref[...] = jnp.zeros(sum_ref.shape, F32) + jnp.sum(jnp.exp(token_score))


def mlp_block(tokens, gain, score_head, near, near_other, far, far_other):
    rows, width = tokens.shape
    shape = (1,) + near.shape[1:]
    near_spec = pl.BlockSpec(shape, lambda s: (jnp.minimum(s, 3), 0, 0))
    far_spec = pl.BlockSpec(shape, lambda s: (jnp.maximum(s - 4, 0), 0, 0))
    whole = pl.BlockSpec((1, width), lambda s: (0, 0))
    return pl.pallas_call(
        mlp_kernel,
        out_shape=(
            jax.ShapeDtypeStruct((rows, width), BF16),
            jax.ShapeDtypeStruct((8, 128), F32),
        ),
        grid=(8,),
        in_specs=[
            pl.BlockSpec((rows, width), lambda s: (0, 0)),
            whole,
            whole,
            near_spec,
            near_spec,
            far_spec,
            far_spec,
        ],
        out_specs=(
            pl.BlockSpec((rows, width), lambda s: (0, 0)),
            pl.BlockSpec((8, 128), lambda s: (0, 0)),
        ),
        scratch_shapes=[pltpu.VMEM((rows, width), BF16), pltpu.VMEM((rows, width), F32)],
        compiler_params=KERNEL_PARAMS,
        cost_estimate=MLP_COST,
    )(
        tokens,
        gain.reshape(1, width),
        score_head.reshape(1, width),
        near,
        near_other,
        far,
        far_other,
    )


def pack_attention_kernel(core_ref, qkv_ref, out_ref, packed_ref):
    depth = qkv_ref.shape[1]
    for member in range(3):
        packed_ref[member * depth : (member + 1) * depth, :] = qkv_ref[member]
    for block in range(depth // 128):
        start = 3 * depth + block * 128
        packed_ref[start : start + 128, :] = out_ref[:, block * 128 : (block + 1) * 128]


def pack_attention(core, qkv, out):
    members, width, local = qkv.shape
    half = width // 2
    return pl.pallas_call(
        pack_attention_kernel,
        out_shape=jax.ShapeDtypeStruct((4 * half, local), BF16),
        grid_spec=pltpu.PrefetchScalarGridSpec(
            num_scalar_prefetch=1,
            grid=(1,),
            in_specs=[
                pl.BlockSpec((members, half, local), lambda s, core_ref: (0, core_ref[0], 0)),
                pl.BlockSpec((local, half), lambda s, core_ref: (0, core_ref[0])),
            ],
            out_specs=pl.BlockSpec((4 * half, local), lambda s, core_ref: (0, 0)),
        ),
    )(core, qkv, out)


def pack_mlp_kernel(core_ref, in_ref, out_ref, packed_ref):
    units = in_ref.shape[1]
    for block in range(in_ref.shape[0] // units):
        rows = slice(block * units, (block + 1) * units)
        packed_ref[:units, rows] = in_ref[rows, :]
    packed_ref[units:, :] = out_ref[...]


def pack_mlp(core, w_in, w_out):
    width, local = w_in.shape
    units = local // 2
    return pl.pallas_call(
        pack_mlp_kernel,
        out_shape=jax.ShapeDtypeStruct((2 * units, width), BF16),
        grid_spec=pltpu.PrefetchScalarGridSpec(
            num_scalar_prefetch=1,
            grid=(1,),
            in_specs=[
                pl.BlockSpec((width, units), lambda s, core_ref: (0, core_ref[0])),
                pl.BlockSpec((units, width), lambda s, core_ref: (core_ref[0], 0)),
            ],
            out_specs=pl.BlockSpec((2 * units, width), lambda s, core_ref: (0, 0)),
        ),
    )(core, w_in, w_out)


def pack_slice(qkv, out, rank, ranks):
    members, width, local = qkv.shape
    blocks = jnp.transpose(out.reshape(local, width // 128, 128), (1, 0, 2)).reshape(1, width, local)
    depth = width // ranks
    joined = jnp.concatenate([qkv, blocks], axis=0)
    return lax.dynamic_slice_in_dim(joined, rank * depth, depth, axis=1).reshape(-1, local)


def shards(
    video,
    gain_space,
    qkv_space,
    out_space,
    gain_time,
    qkv_time,
    out_time,
    gain_mlp,
    w_in,
    w_out,
    score_head,
):
    frames, local_patches, width = video.shape
    patch_count = NX * 2
    clip_ranks = NZ * NCORE
    rows = frames * local_patches
    pairs = local_patches // clip_ranks
    frame_index = lax.axis_index("frame")
    core = frame_index % NCORE
    rank = frame_index % clip_ranks
    core_scalar = core.astype(jnp.int32).reshape(1)
    frame_groups = [[c * clip_ranks + i for i in range(clip_ranks)] for c in range(CLIPS)]
    clip_groups = [[c * 128 + i for i in range(128)] for c in range(CLIPS)]
    rank_groups = [
        [(c * clip_ranks + r) * patch_count + p for c in range(CLIPS) for p in range(patch_count)]
        for r in range(clip_ranks)
    ]

    time_slice = pack_slice(qkv_time, out_time, rank, clip_ranks)
    space_own = pack_attention(core_scalar, qkv_space, out_space)
    mlp_own = pack_mlp(core_scalar, w_in, w_out)
    space_left, space_right = first_phase_x(space_own)
    space_other = first_phase_y(space_own)
    slice_rows = time_slice.size // width
    slices = jnp.broadcast_to(
        time_slice.reshape(1, slice_rows, width), (patch_count, slice_rows, width)
    )
    arrived = lax.all_to_all(
        jnp.concatenate([video, slices], axis=1), "patch", 0, 0, tiled=True
    )
    space_left, space_right, arrived, *space_other = barrier(
        space_left, space_right, arrived, *space_other
    )
    by_frame = jnp.transpose(
        arrived[:, :local_patches].reshape(patch_count, clip_ranks, pairs, width), (1, 0, 2, 3)
    ).reshape(rows, width)
    time_weights = lax.all_gather(
        arrived[:, local_patches:].reshape((patch_count,) + time_slice.shape),
        "frame",
        axis=0,
        axis_index_groups=frame_groups,
    )
    space_far_lo, space_far_hi, space_other_left, space_other_right = second_phase(
        space_left, space_right
    )
    space_near = four(space_own, space_left, space_right, *space_other)
    space_near_other = swap(space_near)
    space_far_lo, space_far_hi, mlp_own = barrier(space_far_lo, space_far_hi, mlp_own)
    space_other_far = third_phase(space_far_lo, space_far_hi)
    mlp_left, mlp_right = first_phase_x(mlp_own)
    space_far = four(
        space_other_left, space_other_right, space_far_lo, space_far_hi, *space_other_far
    )
    space_far, mlp_own = barrier(space_far, mlp_own)
    mlp_other = first_phase_y(mlp_own)
    space_far_other = swap(space_far)
    after_space = space_block(
        core_scalar, by_frame, gain_space, space_near, space_near_other, space_far, space_far_other
    )

    after_space, mlp_left, mlp_right = barrier(after_space, mlp_left, mlp_right)
    mlp_far_lo, mlp_far_hi, mlp_other_left, mlp_other_right = second_phase(mlp_left, mlp_right)
    by_patch = lax.all_to_all(
        after_space, AXES, 0, 0, tiled=True, axis_index_groups=clip_groups
    )
    by_patch, mlp_far_lo, mlp_far_hi = barrier(by_patch, mlp_far_lo, mlp_far_hi)
    mlp_near = four(mlp_own, mlp_left, mlp_right, *mlp_other)
    mlp_near_other = swap(mlp_near)
    mlp_other_far = third_phase(mlp_far_lo, mlp_far_hi)
    after_time = time_block(by_patch, gain_time, time_weights)
    mlp_far = four(mlp_other_left, mlp_other_right, mlp_far_lo, mlp_far_hi, *mlp_other_far)
    after_time, mlp_far = barrier(after_time, mlp_far)
    mlp_far_other = swap(mlp_far)
    at_home = lax.all_to_all(
        after_time, "frame", 0, 0, tiled=True, axis_index_groups=frame_groups
    )
    tokens, sums = mlp_block(
        at_home, gain_mlp, score_head, mlp_near, mlp_near_other, mlp_far, mlp_far_other
    )
    features = jnp.transpose(
        tokens.reshape(clip_ranks, frames, pairs, width), (1, 0, 2, 3)
    ).reshape(frames, local_patches, width)

    def spread(values, axis, groups):
        copies = jnp.broadcast_to(values[None], (16,) + values.shape)
        return lax.all_to_all(copies, axis, 0, 0, tiled=True, axis_index_groups=groups)

    sums = jnp.sum(spread(sums, "frame", frame_groups), axis=0)
    gathered = spread(sums, AXES, rank_groups).reshape((CLIPS, patch_count) + sums.shape)
    per_clip = jnp.sum(gathered[:, :, 0, 0], axis=1)
    score = jnp.log(per_clip / (frames * clip_ranks * local_patches * patch_count))
    return (features, score)


def solution(mesh):
    placed = (
        P("frame", "patch", None),
        P(),
        P(None, None, "patch"),
        P("patch", None),
        P(),
        P(None, None, "patch"),
        P("patch", None),
        P(),
        P(None, "patch"),
        P("patch", None),
        P(),
    )
    return jax.shard_map(
        shards,
        mesh=mesh,
        in_specs=placed,
        out_specs=(P("frame", "patch", None), P()),
        check_vma=False,
    )
```

```python
import functools

import jax
import jax.numpy as jnp
from jax import lax
from jax.experimental import pallas as pl
from jax.experimental.pallas import tpu as pltpu
from jax.sharding import PartitionSpec as P

HDIM = 64
CLIPS = 2
NX, NY, NZ, NCORE = 4, 4, 8, 2
AXES = ("frame", "patch")
BF16 = jnp.bfloat16
F32 = jnp.float32


def place(flat):
    frame, patch = divmod(flat, NX * 2)
    y_hi, rest = divmod(frame, NZ * NCORE)
    z, core = divmod(rest, NCORE)
    y_lo, x = divmod(patch, NX)
    return x, y_hi * 2 + y_lo, z, core


def flat_of(x, y, z, core):
    y_hi, y_lo = divmod(y % NY, 2)
    return ((y_hi * NZ + z % NZ) * NCORE + core % NCORE) * (NX * 2) + y_lo * NX + x % NX


def shift(value, dx=0, dy=0, dz=0, dc=0):
    pairs = []
    for flat in range(NX * NY * NZ * NCORE):
        x, y, z, core = place(flat)
        pairs.append((flat, flat_of(x + dx, y + dy, z + dz, core + dc)))
    return lax.ppermute(value, AXES, pairs)


def dot(left, right):
    return jnp.dot(left, right, preferred_element_type=F32)


def barrier(*values):
    return lax.optimization_barrier(values)


def first_phase_x(own):
    return shift(own, dx=1), shift(own, dx=-1)


def first_phase_y(own):
    cut = own.shape[0] // 2
    return shift(own[:cut], dy=1), shift(own[cut:], dy=-1)


def second_phase(left, right):
    cut = left.shape[0] // 2
    far_lo, far_hi = shift(left[:cut], dx=1), shift(right[cut:], dx=-1)
    return far_lo, far_hi, shift(left, dy=1), shift(right, dy=-1)


def third_phase(far_lo, far_hi):
    return shift(far_lo, dy=1), shift(far_hi, dy=-1)


def join_kernel(count, *refs):
    joined_ref = refs[-1]
    start = 0
    for part in refs[:count]:
        joined_ref[start : start + part.shape[0]] = part[...]
        start += part.shape[0]


def four(*parts, after=()):
    rows = sum(part.shape[0] for part in parts)
    return pl.pallas_call(
        functools.partial(join_kernel, len(parts)),
        out_shape=jax.ShapeDtypeStruct((rows,) + parts[0].shape[1:], BF16),
        in_specs=[pl.BlockSpec(memory_space=pltpu.VMEM)] * len(parts)
        + [pl.BlockSpec(memory_space=pl.ANY)] * len(after),
        compiler_params=pltpu.CompilerParams(vmem_limit_bytes=16 * 2**20),
    )(*parts, *after)


def swap(part):
    return shift(part, dc=1)


def attend(queries, keys, values_in, interleaved):
    tokens = queries.shape[0]
    lane = lax.broadcasted_iota(jnp.int32, (tokens, 2 * HDIM), 1)
    if interleaved:
        row = lax.broadcasted_iota(jnp.int32, (tokens, tokens), 0)
        col = lax.broadcasted_iota(jnp.int32, (tokens, tokens), 1)
        same = (row & 1) == (col & 1)
    contexts = []
    for pair in range(2):
        cols = slice(pair * 2 * HDIM, (pair + 1) * 2 * HDIM)
        q_pair, k_pair, v_pair = queries[:, cols], keys[:, cols], values_in[:, cols]
        results = []
        for head in range(2):
            q_head = jnp.where((lane < HDIM) == (head == 0), q_pair, jnp.zeros_like(q_pair))
            scores = lax.dot_general(
                q_head, k_pair, (((1,), (1,)), ((), ())), preferred_element_type=F32
            )
            if interleaved:
                scores = jnp.where(same, scores, -jnp.inf)
            top = jnp.max(scores, axis=-1, keepdims=True)
            weights = jnp.exp(scores - top)
            denom = jnp.sum(weights, axis=-1, keepdims=True)
            results.append(dot(weights.astype(BF16), v_pair) / denom)
        contexts.append(jnp.where(lane < HDIM, results[0], results[1]).astype(BF16))
    return jnp.concatenate(contexts, axis=1)


def start_norm(tokens, gain_ref, normed_ref, total_ref):
    values = tokens.astype(F32)
    scale = lax.rsqrt(jnp.mean(values * values, axis=-1, keepdims=True) + 1e-06)
    normed_ref[...] = (values * scale * gain_ref[...]).astype(BF16)
    total_ref[...] = values


def add_heads(core_ref, normed_ref, mine_ref, theirs_ref, total_ref, interleaved):
    core = core_ref[0]
    half = normed_ref.shape[1] // 2
    at_mine = pl.multiple_of(core * half, half)
    at_theirs = pl.multiple_of(half - core * half, half)
    x_mine = normed_ref[:, pl.ds(at_mine, half)]
    x_theirs = normed_ref[:, pl.ds(at_theirs, half)]

    def project(member):
        w_mine = jnp.concatenate([mine_ref[0, member], mine_ref[1, member]], axis=1)
        w_theirs = jnp.concatenate([theirs_ref[0, member], theirs_ref[1, member]], axis=1)
        return dot(x_mine, w_mine) + dot(x_theirs, w_theirs)

    queries = (project(0) * HDIM ** (-0.5)).astype(BF16)
    context = attend(queries, project(1).astype(BF16), project(2).astype(BF16), interleaved)
    for ref, start in ((mine_ref, at_mine), (theirs_ref, at_theirs)):
        w_out = row_blocks((ref[0, 3], ref[1, 3]), 0, 128, 4)
        total_ref[:, pl.ds(start, half)] += dot(context, w_out)


def near_kernel(
    core_ref, x_ref, gain_ref, mine_ref, theirs_ref, *rest, interleaved
):
    total_ref, normed_ref = rest[-2:]

    @pl.when(pl.program_id(0) == 0)
    def _():
        unpack = unpack_tokens if interleaved else unpack_frame
        start_norm(unpack(x_ref[...]), gain_ref, normed_ref, total_ref)

    add_heads(core_ref, normed_ref, mine_ref, theirs_ref, total_ref, interleaved)


def far_kernel(
    core_ref, before_ref, normed_ref, mine_ref, theirs_ref, o_ref, total_ref, *, interleaved
):
    step = pl.program_id(0)

    @pl.when(step == 0)
    def _():
        total_ref[...] = before_ref[...]

    add_heads(core_ref, normed_ref, mine_ref, theirs_ref, total_ref, interleaved)

    @pl.when(step == pl.num_programs(0) - 1)
    def _():
        after = total_ref[...].astype(BF16)
        o_ref[...] = after if interleaved else pack_tokens(after)


def unpack_frame(arrived):
    senders, packed, lanes = arrived.shape
    tokens = packed // 8
    blocks = []
    for block in range(8):
        part = arrived[:, block * tokens : (block + 1) * tokens, :]
        blocks.append(part.reshape(senders * tokens, lanes))
    return jnp.concatenate(blocks, axis=1)


def moves(rows, source_of):
    row = lax.broadcasted_iota(jnp.int32, (rows, rows), 0)
    col = lax.broadcasted_iota(jnp.int32, (rows, rows), 1)
    return (source_of(row) == col).astype(F32).astype(BF16)


def pack_tokens(tokens):
    rows, width = tokens.shape
    blocks = width // 128
    by_dest = moves(rows, lambda i: (i // 2 % 8) * 32 + (i // 16) * 2 + i % 2)
    ordered = dot(by_dest, tokens).astype(BF16)
    mix = moves(rows, lambda i: (i // 2 % 8) * 32 + (i // 16) * 2 + i % 2)
    chunks = []
    depth = rows // blocks
    for part in range(blocks):
        piece = ordered[part * depth : (part + 1) * depth]
        stacked = [piece[:, k * 128 : (k + 1) * 128] for k in range(blocks)]
        mixed = dot(mix, jnp.concatenate(stacked, axis=0)).astype(BF16)
        chunks.append(mixed.reshape(rows // 16, 16, 128))
    return jnp.concatenate(chunks, axis=0)


def unpack_tokens(chunks):
    count, deep, lanes = chunks.shape
    rows = count * 2
    blocks = deep // 2
    mix = moves(rows, lambda i: (i // 2 % 16) * 16 + (i // 32) * 2 + i % 2)
    pieces = []
    for part in range(blocks):
        piece = chunks[part * 16 : (part + 1) * 16].reshape(rows, lanes)
        mixed = dot(mix, piece).astype(BF16)
        depth = rows // blocks
        columns = [mixed[k * depth : (k + 1) * depth] for k in range(blocks)]
        pieces.append(jnp.concatenate(columns, axis=1))
    return jnp.concatenate(pieces, axis=0)


ATTENTION_COST = pl.CostEstimate(
    flops=10 * 256 * 2**20, bytes_accessed=10 * 2**20, transcendentals=2**20
)
MLP_COST = pl.CostEstimate(
    flops=16 * 256 * 2**20, bytes_accessed=18 * 2**20, transcendentals=2**20
)
SPACE_COST = pl.CostEstimate(
    flops=5 * 256 * 2**20, bytes_accessed=6 * 2**20, transcendentals=2**19
)
SPACE_PARAMS = pltpu.CompilerParams(vmem_limit_bytes=16 * 2**20)
KERNEL_PARAMS = pltpu.CompilerParams(vmem_limit_bytes=58 * 2**20)


def near_block(core, tokens, gain, mine, theirs, interleaved, after=()):
    width = gain.shape[0]
    shape = tokens.shape if interleaved else (8, tokens.shape[1] // 2, 128)
    rows = shape[0] * shape[1] * shape[2] // width
    whole = (4, 4, width // 2, 128)
    weight_spec = pl.BlockSpec((2,) + whole[1:], lambda s: (s, 0, 0, 0))
    token_spec = pl.BlockSpec((rows, width), lambda s: (0, 0))
    return pl.pallas_call(
        functools.partial(near_kernel, interleaved=interleaved),
        out_shape=(
            jax.ShapeDtypeStruct((rows, width), F32),
            jax.ShapeDtypeStruct((rows, width), BF16),
        ),
        grid=(2,),
        in_specs=[
            pl.BlockSpec(memory_space=pltpu.SMEM),
            pl.BlockSpec(shape, lambda s: (0, 0, 0)),
            pl.BlockSpec((1, width), lambda s: (0, 0)),
            weight_spec,
            weight_spec,
        ]
        + [pl.BlockSpec(memory_space=pl.ANY)] * len(after),
        out_specs=(token_spec, token_spec),
        compiler_params=SPACE_PARAMS,
        cost_estimate=SPACE_COST,
    )(core, tokens, gain.reshape(1, width), mine.reshape(whole), theirs.reshape(whole), *after)


def far_block(core, total, normed, mine, theirs, interleaved):
    rows, width = total.shape
    whole = (4, 4, width // 2, 128)
    weight_spec = pl.BlockSpec((2,) + whole[1:], lambda s: (s, 0, 0, 0))
    token_spec = pl.BlockSpec((rows, width), lambda s: (0, 0))
    shape = (rows, width) if interleaved else (rows // 2, 2 * width // 128, 128)
    return pl.pallas_call(
        functools.partial(far_kernel, interleaved=interleaved),
        out_shape=jax.ShapeDtypeStruct(shape, BF16),
        grid=(2,),
        in_specs=[
            pl.BlockSpec(memory_space=pltpu.SMEM),
            token_spec,
            token_spec,
            weight_spec,
            weight_spec,
        ],
        out_specs=pl.BlockSpec(shape, lambda s: (0,) * len(shape)),
        scratch_shapes=[pltpu.VMEM((rows, width), F32)],
        compiler_params=SPACE_PARAMS,
        cost_estimate=SPACE_COST,
    )(core, total, normed, mine.reshape(whole), theirs.reshape(whole))


def gelu(inner):
    return (0.5 * inner * (1.0 + lax.erf(inner * 2.0 ** (-0.5)))).astype(BF16)


def row_blocks(pair, start, depth, count):
    blocks = []
    for block in range(count):
        rows = slice(start + block * depth, start + (block + 1) * depth)
        blocks.append(jnp.concatenate([part[rows] for part in pair], axis=0))
    return jnp.concatenate(blocks, axis=1)


def mlp_kernel(
    x_ref, gain_ref, head_ref, in_ref, out_ref, o_ref, sum_ref, normed_ref, total_ref
):
    step = pl.program_id(0)
    ranks, shard_count, packed, lanes = in_ref.shape
    width = x_ref.shape[1]
    depth = width // ranks
    units = packed // depth * lanes

    @pl.when(step == 0)
    def _():
        start_norm(x_ref[...], gain_ref, normed_ref, total_ref)

    columns = []
    for shard in range(shard_count):
        for block in range(units // lanes):
            part = in_ref[:, shard, block * depth : (block + 1) * depth, :]
            columns.append(part.reshape(width, lanes))
    hidden = gelu(dot(normed_ref[...], jnp.concatenate(columns, axis=1)))
    depth = units // ranks
    blocks = []
    for block in range(width // lanes):
        shards_of = []
        for shard in range(shard_count):
            part = out_ref[:, shard, block * depth : (block + 1) * depth, :]
            shards_of.append(part.reshape(units, lanes))
        blocks.append(jnp.concatenate(shards_of, axis=0))
    total_ref[...] += dot(hidden, jnp.concatenate(blocks, axis=1))

    @pl.when(step == pl.num_programs(0) - 1)
    def _():
        features = total_ref[...].astype(BF16)
        o_ref[...] = features
        token_score = jnp.sum(features.astype(F32) * head_ref[...], axis=-1, keepdims=True)
        sum_ref[...] = jnp.zeros(sum_ref.shape, F32) + jnp.sum(jnp.exp(token_score))


def mlp_block(tokens, gain, score_head, w_in, w_out):
    rows, width = tokens.shape
    ranks, shard_count, packed, lanes = w_in.shape
    weight_spec = pl.BlockSpec((ranks, 2, packed, lanes), lambda s: (0, s, 0, 0))
    vector = pl.BlockSpec((1, width), lambda s: (0, 0))
    return pl.pallas_call(
        mlp_kernel,
        out_shape=(
            jax.ShapeDtypeStruct((rows, width), BF16),
            jax.ShapeDtypeStruct((8, 128), F32),
        ),
        grid=(shard_count // 2,),
        in_specs=[
            pl.BlockSpec((rows, width), lambda s: (0, 0)),
            vector,
            vector,
            weight_spec,
            weight_spec,
        ],
        out_specs=(
            pl.BlockSpec((rows, width), lambda s: (0, 0)),
            pl.BlockSpec((8, 128), lambda s: (0, 0)),
        ),
        scratch_shapes=[pltpu.VMEM((rows, width), BF16), pltpu.VMEM((rows, width), F32)],
        compiler_params=KERNEL_PARAMS,
        cost_estimate=MLP_COST,
    )(tokens, gain.reshape(1, width), score_head.reshape(1, width), w_in, w_out)


def pack_attention_kernel(core_ref, qkv_ref, out_ref, packed_ref):
    depth = qkv_ref.shape[1]
    for member in range(3):
        packed_ref[member * depth : (member + 1) * depth, :] = qkv_ref[member]
    for block in range(depth // 128):
        start = 3 * depth + block * 128
        packed_ref[start : start + 128, :] = out_ref[:, block * 128 : (block + 1) * 128]


def pack_attention(core, qkv, out):
    members, width, local = qkv.shape
    half = width // 2
    return pl.pallas_call(
        pack_attention_kernel,
        out_shape=jax.ShapeDtypeStruct((4 * half, local), BF16),
        grid_spec=pltpu.PrefetchScalarGridSpec(
            num_scalar_prefetch=1,
            grid=(1,),
            in_specs=[
                pl.BlockSpec((members, half, local), lambda s, core_ref: (0, core_ref[0], 0)),
                pl.BlockSpec((local, half), lambda s, core_ref: (0, core_ref[0])),
            ],
            out_specs=pl.BlockSpec((4 * half, local), lambda s, core_ref: (0, 0)),
        ),
    )(core, qkv, out)


def pack_slice_kernel(rank_ref, in_ref, packed_ref):
    depth = in_ref.shape[0]
    for block in range(in_ref.shape[1] // 128):
        rows = slice(block * depth, (block + 1) * depth)
        for dest in range(packed_ref.shape[0]):
            packed_ref[dest, rows, :] = in_ref[:, block * 128 : (block + 1) * 128]


def pack_slice(rank, w_in, ranks, copies):
    width, units = w_in.shape
    depth = width // ranks
    shape = (copies, depth * units // 128, 128)
    return pl.pallas_call(
        pack_slice_kernel,
        out_shape=jax.ShapeDtypeStruct(shape, BF16),
        grid_spec=pltpu.PrefetchScalarGridSpec(
            num_scalar_prefetch=1,
            grid=(1,),
            in_specs=[pl.BlockSpec((depth, units), lambda s, rank_ref: (rank_ref[0], 0))],
            out_specs=pl.BlockSpec(shape, lambda s, rank_ref: (0, 0, 0)),
        ),
    )(rank, w_in)


def pack_send_kernel(rank_ref, video_ref, out_ref, packed_ref):
    tokens = video_ref.shape[1]
    first = packed_ref.shape[1] // 2
    depth = out_ref.shape[0]
    for block in range(video_ref.shape[2] // 128):
        columns = slice(block * 128, (block + 1) * 128)
        packed_ref[:, block * tokens : (block + 1) * tokens, :] = video_ref[:, :, columns]
        start = first + block * depth
        for dest in range(packed_ref.shape[0]):
            packed_ref[dest, start : start + depth, :] = out_ref[:, columns]


def pack_send(rank, video, w_out, ranks):
    units, width = w_out.shape
    depth = units // ranks
    frames, tokens, _ = video.shape
    shape = (frames, (tokens + depth) * width // 128, 128)
    return pl.pallas_call(
        pack_send_kernel,
        out_shape=jax.ShapeDtypeStruct(shape, BF16),
        grid_spec=pltpu.PrefetchScalarGridSpec(
            num_scalar_prefetch=1,
            grid=(1,),
            in_specs=[
                pl.BlockSpec((frames, tokens, width), lambda s, rank_ref: (0, 0, 0)),
                pl.BlockSpec((depth, width), lambda s, rank_ref: (rank_ref[0], 0)),
            ],
            out_specs=pl.BlockSpec(shape, lambda s, rank_ref: (0, 0, 0)),
        ),
    )(rank, video, w_out)


def shards(
    video,
    gain_space,
    qkv_space,
    out_space,
    gain_time,
    qkv_time,
    out_time,
    gain_mlp,
    w_in,
    w_out,
    score_head,
):
    frames, local_patches, width = video.shape
    patch_count = NX * 2
    clip_ranks = NZ * NCORE
    rows = frames * local_patches
    pairs = local_patches // clip_ranks
    frame_index = lax.axis_index("frame")
    core = frame_index % NCORE
    rank = frame_index % clip_ranks
    core_scalar = core.astype(jnp.int32).reshape(1)
    frame_groups = [[c * clip_ranks + i for i in range(clip_ranks)] for c in range(CLIPS)]
    clip_groups = [[c * 128 + i for i in range(128)] for c in range(CLIPS)]
    rank_groups = [
        [(c * clip_ranks + r) * patch_count + p for c in range(CLIPS) for p in range(patch_count)]
        for r in range(clip_ranks)
    ]

    space_own = pack_attention(core_scalar, qkv_space, out_space)
    space_own, video, rank_scalar = barrier(space_own, video, rank.astype(jnp.int32).reshape(1))
    space_left, space_right = first_phase_x(space_own)
    space_other = first_phase_y(space_own)
    def over_frame(slices):
        return lax.all_gather(slices, "frame", axis=0, axis_index_groups=frame_groups)

    in_slices = lax.all_to_all(
        pack_slice(rank_scalar, w_in, clip_ranks, patch_count), "patch", 0, 0, tiled=True
    )
    packed = pack_send(rank_scalar, video, w_out, clip_ranks)
    time_own = pack_attention(core_scalar, qkv_time, out_time)
    space_left, space_right, in_slices, packed, *space_other = barrier(
        space_left, space_right, in_slices, packed, *space_other
    )
    gathered_in = over_frame(in_slices)
    arrived = lax.all_to_all(packed, "patch", 0, 0, tiled=True)
    second = second_phase(space_left, space_right)
    (
        space_far_lo, space_far_hi, space_other_left, space_other_right, space_own, time_own,
        arrived,
    ) = barrier(*second, space_own, time_own, arrived)
    gathered_out = over_frame(arrived[:, arrived.shape[1] // 2 :])
    space_other_far = third_phase(space_far_lo, space_far_hi)
    time_left, time_right = first_phase_x(time_own)
    space_near = four(space_own, space_left, space_right, *space_other)
    space_near_other = swap(space_near)
    total, normed = near_block(
        core_scalar,
        arrived,
        gain_space,
        space_near,
        space_near_other,
        False,
        after=(time_left, time_right),
    )
    space_far = four(
        space_other_left,
        space_other_right,
        space_far_lo,
        space_far_hi,
        *space_other_far,
        after=(total,),
    )
    space_far_other = swap(space_far)
    time_other = shift(time_own, dy=1)
    after_space = far_block(core_scalar, total, normed, space_far, space_far_other, False)

    time_far, time_other_left = shift(time_left, dx=1), shift(time_left, dy=1)
    time_other_right = shift(time_right, dy=-1)
    time_other_far = shift(time_own, dx=2, dy=-1)
    by_patch = lax.all_to_all(after_space, AXES, 0, 0, tiled=True, axis_index_groups=clip_groups)
    time_near = four(time_own, time_left, time_right, time_other, after=(after_space,))
    time_near_other = swap(time_near)
    time_far = four(
        time_other_far, time_far, time_other_left, time_other_right, after=(by_patch,)
    )
    time_far_other = swap(time_far)
    total, normed = near_block(
        core_scalar, by_patch, gain_time, time_near, time_near_other, True
    )
    after_time = far_block(core_scalar, total, normed, time_far, time_far_other, True)
    at_home = lax.all_to_all(
        after_time, "frame", 0, 0, tiled=True, axis_index_groups=frame_groups
    )
    tokens, sums = mlp_block(at_home, gain_mlp, score_head, gathered_in, gathered_out)
    features = jnp.transpose(
        tokens.reshape(clip_ranks, frames, pairs, width), (1, 0, 2, 3)
    ).reshape(frames, local_patches, width)

    def spread(values, axis, groups):
        copies = jnp.broadcast_to(values[None], (16,) + values.shape)
        return lax.all_to_all(copies, axis, 0, 0, tiled=True, axis_index_groups=groups)

    sums = jnp.sum(spread(sums, "frame", frame_groups), axis=0)
    gathered = spread(sums, AXES, rank_groups).reshape((CLIPS, patch_count) + sums.shape)
    per_clip = jnp.sum(gathered[:, :, 0, 0], axis=1)
    score = jnp.log(per_clip / (frames * clip_ranks * local_patches * patch_count))
    return (features, score)


def solution(mesh):
    placed = (
        P("frame", "patch", None),
        P(),
        P(None, None, "patch"),
        P("patch", None),
        P(),
        P(None, None, "patch"),
        P("patch", None),
        P(),
        P(None, "patch"),
        P("patch", None),
        P(),
    )
    return jax.shard_map(
        shards,
        mesh=mesh,
        in_specs=placed,
        out_specs=(P("frame", "patch", None), P()),
        check_vma=False,
    )
```

```python
import functools

import jax
import jax.numpy as jnp
from jax import lax
from jax.experimental import pallas as pl
from jax.experimental.pallas import tpu as pltpu
from jax.sharding import PartitionSpec as P

HDIM = 64
CLIPS = 2
NX, NY, NZ, NCORE = 4, 4, 8, 2
AXES = ("frame", "patch")
BF16 = jnp.bfloat16
F32 = jnp.float32


def place(flat):
    frame, patch = divmod(flat, NX * 2)
    y_hi, rest = divmod(frame, NZ * NCORE)
    z, core = divmod(rest, NCORE)
    y_lo, x = divmod(patch, NX)
    return x, y_hi * 2 + y_lo, z, core


def flat_of(x, y, z, core):
    y_hi, y_lo = divmod(y % NY, 2)
    return ((y_hi * NZ + z % NZ) * NCORE + core % NCORE) * (NX * 2) + y_lo * NX + x % NX


def shift(value, dx=0, dy=0, dz=0, dc=0):
    pairs = []
    for flat in range(NX * NY * NZ * NCORE):
        x, y, z, core = place(flat)
        pairs.append((flat, flat_of(x + dx, y + dy, z + dz, core + dc)))
    return lax.ppermute(value, AXES, pairs)


def dot(left, right):
    return jnp.dot(left, right, preferred_element_type=F32)


def barrier(*values):
    return lax.optimization_barrier(values)


def first_phase_x(own):
    return shift(own, dx=1), shift(own, dx=-1)


def first_phase_y(own):
    cut = own.shape[0] // 2
    return shift(own[:cut], dy=1), shift(own[cut:], dy=-1)


def second_phase(left, right):
    cut = left.shape[0] // 2
    far_lo, far_hi = shift(left[:cut], dx=1), shift(right[cut:], dx=-1)
    return far_lo, far_hi, shift(left, dy=1), shift(right, dy=-1)


def third_phase(far_lo, far_hi):
    return shift(far_lo, dy=1), shift(far_hi, dy=-1)


def join_kernel(count, *refs):
    joined_ref, sems = refs[-2:]
    copies = []
    start = 0
    for at, part in enumerate(refs[:count]):
        rows = pl.ds(start, part.shape[0])
        copies.append(pltpu.make_async_copy(part, joined_ref.at[rows], sems.at[at]))
        start += part.shape[0]
    for copy in copies:
        copy.start()
    for copy in copies:
        copy.wait()


def four(*parts, after=()):
    rows = sum(part.shape[0] for part in parts)
    return pl.pallas_call(
        functools.partial(join_kernel, len(parts)),
        out_shape=jax.ShapeDtypeStruct((rows,) + parts[0].shape[1:], BF16),
        in_specs=[pl.BlockSpec(memory_space=pl.ANY)] * (len(parts) + len(after)),
        out_specs=pl.BlockSpec(memory_space=pltpu.VMEM),
        scratch_shapes=[pltpu.SemaphoreType.DMA((len(parts),))],
        compiler_params=pltpu.CompilerParams(vmem_limit_bytes=16 * 2**20),
    )(*parts, *after)


def swap(part):
    return shift(part, dc=1)


def attend(queries, keys, values_in, interleaved):
    tokens = queries.shape[0]
    lane = lax.broadcasted_iota(jnp.int32, (tokens, 2 * HDIM), 1)
    if interleaved:
        row = lax.broadcasted_iota(jnp.int32, (tokens, tokens), 0)
        col = lax.broadcasted_iota(jnp.int32, (tokens, tokens), 1)
        same = (row & 1) == (col & 1)
    contexts = []
    for pair in range(2):
        cols = slice(pair * 2 * HDIM, (pair + 1) * 2 * HDIM)
        q_pair, k_pair, v_pair = queries[:, cols], keys[:, cols], values_in[:, cols]
        results = []
        for head in range(2):
            q_head = jnp.where((lane < HDIM) == (head == 0), q_pair, jnp.zeros_like(q_pair))
            scores = lax.dot_general(
                q_head, k_pair, (((1,), (1,)), ((), ())), preferred_element_type=F32
            )
            if interleaved:
                scores = jnp.where(same, scores, -jnp.inf)
            top = jnp.max(scores, axis=-1, keepdims=True)
            weights = jnp.exp(scores - top)
            denom = jnp.sum(weights, axis=-1, keepdims=True)
            results.append(dot(weights.astype(BF16), v_pair) / denom)
        contexts.append(jnp.where(lane < HDIM, results[0], results[1]).astype(BF16))
    return jnp.concatenate(contexts, axis=1)


def start_norm(tokens, gain_ref, normed_ref, total_ref):
    values = tokens.astype(F32)
    scale = lax.rsqrt(jnp.mean(values * values, axis=-1, keepdims=True) + 1e-06)
    normed_ref[...] = (values * scale * gain_ref[...]).astype(BF16)
    total_ref[...] = values


def add_heads(core_ref, normed_ref, mine_ref, theirs_ref, total_ref, interleaved):
    core = core_ref[0]
    half = normed_ref.shape[1] // 2
    at_mine = pl.multiple_of(core * half, half)
    at_theirs = pl.multiple_of(half - core * half, half)
    x_mine = normed_ref[:, pl.ds(at_mine, half)]
    x_theirs = normed_ref[:, pl.ds(at_theirs, half)]

    def project(member):
        w_mine = jnp.concatenate([mine_ref[0, member], mine_ref[1, member]], axis=1)
        w_theirs = jnp.concatenate([theirs_ref[0, member], theirs_ref[1, member]], axis=1)
        return dot(x_mine, w_mine) + dot(x_theirs, w_theirs)

    queries = (project(0) * HDIM ** (-0.5)).astype(BF16)
    context = attend(queries, project(1).astype(BF16), project(2).astype(BF16), interleaved)
    for ref, start in ((mine_ref, at_mine), (theirs_ref, at_theirs)):
        w_out = row_blocks((ref[0, 3], ref[1, 3]), 0, 128, 4)
        total_ref[:, pl.ds(start, half)] += dot(context, w_out)


def near_kernel(
    core_ref, x_ref, gain_ref, mine_ref, theirs_ref, *rest, interleaved
):
    total_ref, normed_ref = rest[-2:]

    @pl.when(pl.program_id(0) == 0)
    def _():
        unpack = unpack_tokens if interleaved else unpack_frame
        start_norm(unpack(x_ref[...]), gain_ref, normed_ref, total_ref)

    add_heads(core_ref, normed_ref, mine_ref, theirs_ref, total_ref, interleaved)


def far_kernel(
    core_ref, before_ref, normed_ref, mine_ref, theirs_ref, o_ref, total_ref, *, interleaved
):
    step = pl.program_id(0)

    @pl.when(step == 0)
    def _():
        total_ref[...] = before_ref[...]

    add_heads(core_ref, normed_ref, mine_ref, theirs_ref, total_ref, interleaved)

    @pl.when(step == pl.num_programs(0) - 1)
    def _():
        after = total_ref[...].astype(BF16)
        o_ref[...] = after if interleaved else pack_tokens(after)


def unpack_frame(arrived):
    senders, packed, lanes = arrived.shape
    tokens = packed // 8
    blocks = []
    for block in range(8):
        part = arrived[:, block * tokens : (block + 1) * tokens, :]
        blocks.append(part.reshape(senders * tokens, lanes))
    return jnp.concatenate(blocks, axis=1)


def moves(rows, source_of):
    row = lax.broadcasted_iota(jnp.int32, (rows, rows), 0)
    col = lax.broadcasted_iota(jnp.int32, (rows, rows), 1)
    return (source_of(row) == col).astype(F32).astype(BF16)


def pack_tokens(tokens):
    rows, width = tokens.shape
    blocks = width // 128
    by_dest = moves(rows, lambda i: (i // 2 % 8) * 32 + (i // 16) * 2 + i % 2)
    ordered = dot(by_dest, tokens).astype(BF16)
    mix = moves(rows, lambda i: (i // 2 % 8) * 32 + (i // 16) * 2 + i % 2)
    chunks = []
    depth = rows // blocks
    for part in range(blocks):
        piece = ordered[part * depth : (part + 1) * depth]
        stacked = [piece[:, k * 128 : (k + 1) * 128] for k in range(blocks)]
        mixed = dot(mix, jnp.concatenate(stacked, axis=0)).astype(BF16)
        chunks.append(mixed.reshape(rows // 16, 16, 128))
    return jnp.concatenate(chunks, axis=0)


def unpack_tokens(chunks):
    count, deep, lanes = chunks.shape
    rows = count * 2
    blocks = deep // 2
    mix = moves(rows, lambda i: (i // 2 % 16) * 16 + (i // 32) * 2 + i % 2)
    pieces = []
    for part in range(blocks):
        piece = chunks[part * 16 : (part + 1) * 16].reshape(rows, lanes)
        mixed = dot(mix, piece).astype(BF16)
        depth = rows // blocks
        columns = [mixed[k * depth : (k + 1) * depth] for k in range(blocks)]
        pieces.append(jnp.concatenate(columns, axis=1))
    return jnp.concatenate(pieces, axis=0)


ATTENTION_COST = pl.CostEstimate(
    flops=10 * 256 * 2**20, bytes_accessed=10 * 2**20, transcendentals=2**20
)
MLP_COST = pl.CostEstimate(
    flops=16 * 256 * 2**20, bytes_accessed=18 * 2**20, transcendentals=2**20
)
SPACE_COST = pl.CostEstimate(
    flops=5 * 256 * 2**20, bytes_accessed=6 * 2**20, transcendentals=2**19
)
SPACE_PARAMS = pltpu.CompilerParams(vmem_limit_bytes=16 * 2**20)
KERNEL_PARAMS = pltpu.CompilerParams(vmem_limit_bytes=58 * 2**20)


def near_block(core, tokens, gain, mine, theirs, interleaved, after=()):
    width = gain.shape[0]
    shape = tokens.shape if interleaved else (8, tokens.shape[1] // 2, 128)
    rows = shape[0] * shape[1] * shape[2] // width
    whole = (4, 4, width // 2, 128)
    weight_spec = pl.BlockSpec((2,) + whole[1:], lambda s: (s, 0, 0, 0))
    token_spec = pl.BlockSpec((rows, width), lambda s: (0, 0))
    return pl.pallas_call(
        functools.partial(near_kernel, interleaved=interleaved),
        out_shape=(
            jax.ShapeDtypeStruct((rows, width), F32),
            jax.ShapeDtypeStruct((rows, width), BF16),
        ),
        grid=(2,),
        in_specs=[
            pl.BlockSpec(memory_space=pltpu.SMEM),
            pl.BlockSpec(shape, lambda s: (0, 0, 0)),
            pl.BlockSpec((1, width), lambda s: (0, 0)),
            weight_spec,
            weight_spec,
        ]
        + [pl.BlockSpec(memory_space=pl.ANY)] * len(after),
        out_specs=(token_spec, token_spec),
        compiler_params=SPACE_PARAMS,
        cost_estimate=SPACE_COST,
    )(core, tokens, gain.reshape(1, width), mine.reshape(whole), theirs.reshape(whole), *after)


def far_block(core, total, normed, mine, theirs, interleaved):
    rows, width = total.shape
    whole = (4, 4, width // 2, 128)
    weight_spec = pl.BlockSpec((2,) + whole[1:], lambda s: (s, 0, 0, 0))
    token_spec = pl.BlockSpec((rows, width), lambda s: (0, 0))
    shape = (rows, width) if interleaved else (rows // 2, 2 * width // 128, 128)
    return pl.pallas_call(
        functools.partial(far_kernel, interleaved=interleaved),
        out_shape=jax.ShapeDtypeStruct(shape, BF16),
        grid=(2,),
        in_specs=[
            pl.BlockSpec(memory_space=pltpu.SMEM),
            token_spec,
            token_spec,
            weight_spec,
            weight_spec,
        ],
        out_specs=pl.BlockSpec(shape, lambda s: (0,) * len(shape)),
        scratch_shapes=[pltpu.VMEM((rows, width), F32)],
        compiler_params=SPACE_PARAMS,
        cost_estimate=SPACE_COST,
    )(core, total, normed, mine.reshape(whole), theirs.reshape(whole))


def gelu(inner):
    return (0.5 * inner * (1.0 + lax.erf(inner * 2.0 ** (-0.5)))).astype(BF16)


def row_blocks(pair, start, depth, count):
    blocks = []
    for block in range(count):
        rows = slice(start + block * depth, start + (block + 1) * depth)
        blocks.append(jnp.concatenate([part[rows] for part in pair], axis=0))
    return jnp.concatenate(blocks, axis=1)


def hidden_kernel(x_ref, gain_ref, in_ref, o_ref, normed_ref):
    ranks, shard_count, packed, lanes = in_ref.shape
    width = x_ref.shape[1]
    depth = width // ranks

    @pl.when(pl.program_id(0) == 0)
    def _():
        values = x_ref[...].astype(F32)
        scale = lax.rsqrt(jnp.mean(values * values, axis=-1, keepdims=True) + 1e-06)
        normed_ref[...] = (values * scale * gain_ref[...]).astype(BF16)

    columns = []
    for shard in range(shard_count):
        for block in range(packed // depth):
            part = in_ref[:, shard, block * depth : (block + 1) * depth, :]
            columns.append(part.reshape(width, lanes))
    o_ref[...] = gelu(dot(normed_ref[...], jnp.concatenate(columns, axis=1)))


def hidden_block(tokens, gain, w_in):
    rows, width = tokens.shape
    ranks, shard_count, packed, lanes = w_in.shape
    units = packed * ranks * lanes // width
    return pl.pallas_call(
        hidden_kernel,
        out_shape=jax.ShapeDtypeStruct((rows, shard_count * units), BF16),
        grid=(shard_count // 2,),
        in_specs=[
            pl.BlockSpec((rows, width), lambda s: (0, 0)),
            pl.BlockSpec((1, width), lambda s: (0, 0)),
            pl.BlockSpec((ranks, 2, packed, lanes), lambda s: (0, s, 0, 0)),
        ],
        out_specs=pl.BlockSpec((rows, 2 * units), lambda s: (0, s)),
        scratch_shapes=[pltpu.VMEM((rows, width), BF16)],
        compiler_params=KERNEL_PARAMS,
        cost_estimate=MLP_COST,
    )(tokens, gain.reshape(1, width), w_in)


def mlp_kernel(x_ref, head_ref, hidden_ref, out_ref, o_ref, total_ref):
    step = pl.program_id(0)
    ranks, shard_count, packed, lanes = out_ref.shape
    width = x_ref.shape[1]
    units = hidden_ref.shape[1] // shard_count

    @pl.when(step == 0)
    def _():
        total_ref[...] = x_ref[...].astype(F32)

    depth = units // ranks
    blocks = []
    for block in range(width // lanes):
        shards_of = []
        for shard in range(shard_count):
            part = out_ref[:, shard, block * depth : (block + 1) * depth, :]
            shards_of.append(part.reshape(units, lanes))
        blocks.append(jnp.concatenate(shards_of, axis=0))
    total_ref[...] += dot(hidden_ref[...], jnp.concatenate(blocks, axis=1))

    @pl.when(step == pl.num_programs(0) - 1)
    def _():
        features = total_ref[...].astype(BF16)
        dests = o_ref.shape[0]
        rows = features.shape[0] // dests
        for block in range(width // lanes):
            part = features[:, block * lanes : (block + 1) * lanes]
            o_ref[:, block * rows : (block + 1) * rows, :] = part.reshape(dests, rows, lanes)
        token_score = jnp.sum(features.astype(F32) * head_ref[...], axis=-1, keepdims=True)
        rest = jnp.zeros((rows, lanes), F32) + jnp.sum(jnp.exp(token_score))
        row = lax.broadcasted_iota(jnp.int32, (rows, lanes), 0)
        terms = jnp.zeros((rows, lanes), F32)
        for term in range(3):
            rounded = rest.astype(BF16).astype(F32)
            terms = jnp.where(row == term, rounded, terms)
            rest = rest - rounded
        last = rows * (width // lanes)
        for dest in range(dests):
            o_ref[dest, last:, :] = terms.astype(BF16)


def unpack_kernel(chunks_ref, o_ref):
    senders, rows, lanes = chunks_ref.shape
    per_block = rows // 9
    blocks = []
    for block in range(8):
        part = chunks_ref[:, block * per_block : (block + 1) * per_block, :]
        blocks.append(part.reshape(senders * per_block, lanes))
    order = moves(
        senders * per_block,
        lambda i: (i // 2 % senders) * per_block + (i // (2 * senders)) * 2 + i % 2,
    )
    o_ref[...] = dot(order, jnp.concatenate(blocks, axis=1)).astype(BF16)


def unpack_features(chunks, width):
    senders, rows, lanes = chunks.shape
    return pl.pallas_call(
        unpack_kernel,
        out_shape=jax.ShapeDtypeStruct((senders * rows // 9, width), BF16),
        compiler_params=pltpu.CompilerParams(vmem_limit_bytes=16 * 2**20),
    )(chunks)


def mlp_block(tokens, hidden, score_head, w_out):
    rows, width = tokens.shape
    ranks, shard_count, packed, lanes = w_out.shape
    shape = (ranks, rows // ranks * (width // lanes + 1), lanes)
    return pl.pallas_call(
        mlp_kernel,
        out_shape=jax.ShapeDtypeStruct(shape, BF16),
        grid=(shard_count // 2,),
        in_specs=[
            pl.BlockSpec((rows, width), lambda s: (0, 0)),
            pl.BlockSpec((1, width), lambda s: (0, 0)),
            pl.BlockSpec((rows, 2 * hidden.shape[1] // shard_count), lambda s: (0, s)),
            pl.BlockSpec((ranks, 2, packed, lanes), lambda s: (0, s, 0, 0)),
        ],
        out_specs=pl.BlockSpec(shape, lambda s: (0, 0, 0)),
        scratch_shapes=[pltpu.VMEM((rows, width), F32)],
        compiler_params=KERNEL_PARAMS,
        cost_estimate=MLP_COST,
    )(tokens, score_head.reshape(1, width), hidden, w_out)


def pack_attention_kernel(core_ref, qkv_ref, out_ref, packed_ref):
    depth = qkv_ref.shape[1]
    for member in range(3):
        packed_ref[member * depth : (member + 1) * depth, :] = qkv_ref[member]
    for block in range(depth // 128):
        start = 3 * depth + block * 128
        packed_ref[start : start + 128, :] = out_ref[:, block * 128 : (block + 1) * 128]


def pack_attention(core, qkv, out):
    members, width, local = qkv.shape
    half = width // 2
    return pl.pallas_call(
        pack_attention_kernel,
        out_shape=jax.ShapeDtypeStruct((4 * half, local), BF16),
        grid_spec=pltpu.PrefetchScalarGridSpec(
            num_scalar_prefetch=1,
            grid=(1,),
            in_specs=[
                pl.BlockSpec((members, half, local), lambda s, core_ref: (0, core_ref[0], 0)),
                pl.BlockSpec((local, half), lambda s, core_ref: (0, core_ref[0])),
            ],
            out_specs=pl.BlockSpec((4 * half, local), lambda s, core_ref: (0, 0)),
        ),
    )(core, qkv, out)


def pack_slice_kernel(rank_ref, in_ref, packed_ref):
    depth = in_ref.shape[0]
    for block in range(in_ref.shape[1] // 128):
        rows = slice(block * depth, (block + 1) * depth)
        for dest in range(packed_ref.shape[0]):
            packed_ref[dest, rows, :] = in_ref[:, block * 128 : (block + 1) * 128]


def pack_slice(rank, w_in, ranks, copies):
    width, units = w_in.shape
    depth = width // ranks
    shape = (copies, depth * units // 128, 128)
    return pl.pallas_call(
        pack_slice_kernel,
        out_shape=jax.ShapeDtypeStruct(shape, BF16),
        grid_spec=pltpu.PrefetchScalarGridSpec(
            num_scalar_prefetch=1,
            grid=(1,),
            in_specs=[pl.BlockSpec((depth, units), lambda s, rank_ref: (rank_ref[0], 0))],
            out_specs=pl.BlockSpec(shape, lambda s, rank_ref: (0, 0, 0)),
        ),
    )(rank, w_in)


def pack_send_kernel(rank_ref, video_ref, out_ref, packed_ref):
    tokens = video_ref.shape[1]
    first = packed_ref.shape[1] // 2
    depth = out_ref.shape[0]
    for block in range(video_ref.shape[2] // 128):
        columns = slice(block * 128, (block + 1) * 128)
        packed_ref[:, block * tokens : (block + 1) * tokens, :] = video_ref[:, :, columns]
        start = first + block * depth
        for dest in range(packed_ref.shape[0]):
            packed_ref[dest, start : start + depth, :] = out_ref[:, columns]


def pack_send(rank, video, w_out, ranks):
    units, width = w_out.shape
    depth = units // ranks
    frames, tokens, _ = video.shape
    shape = (frames, (tokens + depth) * width // 128, 128)
    return pl.pallas_call(
        pack_send_kernel,
        out_shape=jax.ShapeDtypeStruct(shape, BF16),
        grid_spec=pltpu.PrefetchScalarGridSpec(
            num_scalar_prefetch=1,
            grid=(1,),
            in_specs=[
                pl.BlockSpec((frames, tokens, width), lambda s, rank_ref: (0, 0, 0)),
                pl.BlockSpec((depth, width), lambda s, rank_ref: (rank_ref[0], 0)),
            ],
            out_specs=pl.BlockSpec(shape, lambda s, rank_ref: (0, 0, 0)),
        ),
    )(rank, video, w_out)


def shards(
    video,
    gain_space,
    qkv_space,
    out_space,
    gain_time,
    qkv_time,
    out_time,
    gain_mlp,
    w_in,
    w_out,
    score_head,
):
    frames, local_patches, width = video.shape
    patch_count = NX * 2
    clip_ranks = NZ * NCORE
    rows = frames * local_patches
    pairs = local_patches // clip_ranks
    frame_index = lax.axis_index("frame")
    core = frame_index % NCORE
    rank = frame_index % clip_ranks
    core_scalar = core.astype(jnp.int32).reshape(1)
    frame_groups = [[c * clip_ranks + i for i in range(clip_ranks)] for c in range(CLIPS)]
    clip_groups = [[c * 128 + i for i in range(128)] for c in range(CLIPS)]
    rank_groups = [
        [(c * clip_ranks + r) * patch_count + p for c in range(CLIPS) for p in range(patch_count)]
        for r in range(clip_ranks)
    ]

    space_own = pack_attention(core_scalar, qkv_space, out_space)
    space_own, video, rank_scalar = barrier(space_own, video, rank.astype(jnp.int32).reshape(1))
    space_left, space_right = first_phase_x(space_own)
    space_other = first_phase_y(space_own)
    def over_frame(slices):
        return lax.all_gather(slices, "frame", axis=0, axis_index_groups=frame_groups)

    in_slices = lax.all_to_all(
        pack_slice(rank_scalar, w_in, clip_ranks, patch_count), "patch", 0, 0, tiled=True
    )
    packed = pack_send(rank_scalar, video, w_out, clip_ranks)
    time_own = pack_attention(core_scalar, qkv_time, out_time)
    space_left, space_right, in_slices, packed, *space_other = barrier(
        space_left, space_right, in_slices, packed, *space_other
    )
    gathered_in = over_frame(in_slices)
    arrived = lax.all_to_all(packed, "patch", 0, 0, tiled=True)
    second = second_phase(space_left, space_right)
    (
        space_far_lo, space_far_hi, space_other_left, space_other_right, space_own, time_own,
        arrived,
    ) = barrier(*second, space_own, time_own, arrived)
    gathered_out = over_frame(arrived[:, arrived.shape[1] // 2 :])
    space_other_far = third_phase(space_far_lo, space_far_hi)
    time_left, time_right = first_phase_x(time_own)
    space_near = four(space_own, space_left, space_right, *space_other)
    space_near_other = swap(space_near)
    total, normed = near_block(
        core_scalar,
        arrived,
        gain_space,
        space_near,
        space_near_other,
        False,
        after=(time_left, time_right),
    )
    space_far = four(
        space_other_left,
        space_other_right,
        space_far_lo,
        space_far_hi,
        *space_other_far,
        after=(total,),
    )
    space_far_other = swap(space_far)
    time_other = shift(time_own, dy=1)
    after_space = far_block(core_scalar, total, normed, space_far, space_far_other, False)

    time_far, time_other_left = shift(time_left, dx=1), shift(time_left, dy=1)
    time_other_right = shift(time_right, dy=-1)
    time_other_far = shift(time_own, dx=2, dy=-1)
    by_patch = lax.all_to_all(after_space, AXES, 0, 0, tiled=True, axis_index_groups=clip_groups)
    time_near = four(time_own, time_left, time_right, time_other, after=(after_space,))
    time_near_other = swap(time_near)
    time_far = four(
        time_other_far, time_far, time_other_left, time_other_right, after=(by_patch,)
    )
    time_far_other = swap(time_far)
    total, normed = near_block(
        core_scalar, by_patch, gain_time, time_near, time_near_other, True
    )
    after_time = far_block(core_scalar, total, normed, time_far, time_far_other, True)
    hidden = hidden_block(after_time, gain_mlp, gathered_in)
    chunks = mlp_block(after_time, hidden, score_head, gathered_out)
    at_home = lax.all_to_all(
        chunks, "frame", 0, 0, tiled=True, axis_index_groups=frame_groups
    )
    last = at_home.shape[1] // 9 * 8
    part_sum = jnp.sum(at_home[:, last:, 0].astype(F32))
    sums = lax.all_to_all(
        jnp.broadcast_to(part_sum, (16, 8, 128)),
        AXES,
        0,
        0,
        tiled=True,
        axis_index_groups=rank_groups,
    )
    features = unpack_features(at_home, width).reshape(frames, local_patches, width)
    per_clip = jnp.sum(sums[:, 0, 0].reshape(CLIPS, patch_count), axis=1)
    score = jnp.log(per_clip / (frames * clip_ranks * local_patches * patch_count))
    return (features, score)


def solution(mesh):
    placed = (
        P("frame", "patch", None),
        P(),
        P(None, None, "patch"),
        P("patch", None),
        P(),
        P(None, None, "patch"),
        P("patch", None),
        P(),
        P(None, "patch"),
        P("patch", None),
        P(),
    )
    return jax.shard_map(
        shards,
        mesh=mesh,
        in_specs=placed,
        out_specs=(P("frame", "patch", None), P()),
        check_vma=False,
    )
```

```python
import functools

import jax
import jax.numpy as jnp
from jax import lax
from jax.experimental import pallas as pl
from jax.experimental.pallas import tpu as pltpu
from jax.sharding import PartitionSpec as P

HDIM = 64
CLIPS = 2
NX, NY, NZ, NCORE = 4, 4, 8, 2
AXES = ("frame", "patch")
BF16 = jnp.bfloat16
F32 = jnp.float32


def place(flat):
    frame, patch = divmod(flat, NX * 2)
    y_hi, rest = divmod(frame, NZ * NCORE)
    z, core = divmod(rest, NCORE)
    y_lo, x = divmod(patch, NX)
    return x, y_hi * 2 + y_lo, z, core


def flat_of(x, y, z, core):
    y_hi, y_lo = divmod(y % NY, 2)
    return ((y_hi * NZ + z % NZ) * NCORE + core % NCORE) * (NX * 2) + y_lo * NX + x % NX


def shift(value, dx=0, dy=0, dz=0, dc=0):
    pairs = []
    for flat in range(NX * NY * NZ * NCORE):
        x, y, z, core = place(flat)
        pairs.append((flat, flat_of(x + dx, y + dy, z + dz, core + dc)))
    return lax.ppermute(value, AXES, pairs)


def dot(left, right):
    return jnp.dot(left, right, preferred_element_type=F32)


def barrier(*values):
    return lax.optimization_barrier(values)


def first_phase_x(own):
    return shift(own, dx=1), shift(own, dx=-1)


def first_phase_y(own):
    cut = own.shape[0] // 2
    return shift(own[:cut], dy=1), shift(own[cut:], dy=-1)


def second_phase(left, right):
    cut = left.shape[0] // 2
    far_lo, far_hi = shift(left[:cut], dx=1), shift(right[cut:], dx=-1)
    return far_lo, far_hi, shift(left, dy=1), shift(right, dy=-1)


def third_phase(far_lo, far_hi):
    return shift(far_lo, dy=1), shift(far_hi, dy=-1)


def join_kernel(count, *refs):
    joined_ref, sems = refs[-2:]
    copies = []
    start = 0
    for at, part in enumerate(refs[:count]):
        rows = pl.ds(start, part.shape[0])
        copies.append(pltpu.make_async_copy(part, joined_ref.at[rows], sems.at[at]))
        start += part.shape[0]
    for copy in copies:
        copy.start()
    for copy in copies:
        copy.wait()


def four(*parts, after=()):
    rows = sum(part.shape[0] for part in parts)
    return pl.pallas_call(
        functools.partial(join_kernel, len(parts)),
        out_shape=jax.ShapeDtypeStruct((rows,) + parts[0].shape[1:], BF16),
        in_specs=[pl.BlockSpec(memory_space=pl.ANY)] * (len(parts) + len(after)),
        out_specs=pl.BlockSpec(memory_space=pltpu.VMEM),
        scratch_shapes=[pltpu.SemaphoreType.DMA((len(parts),))],
        compiler_params=pltpu.CompilerParams(vmem_limit_bytes=16 * 2**20),
    )(*parts, *after)


def swap(part):
    return shift(part, dc=1)


def attend(queries, keys, values_in, interleaved):
    tokens = queries.shape[0]
    lane = lax.broadcasted_iota(jnp.int32, (tokens, 2 * HDIM), 1)
    if interleaved:
        row = lax.broadcasted_iota(jnp.int32, (tokens, tokens), 0)
        col = lax.broadcasted_iota(jnp.int32, (tokens, tokens), 1)
        same = (row & 1) == (col & 1)
    contexts = []
    for pair in range(2):
        cols = slice(pair * 2 * HDIM, (pair + 1) * 2 * HDIM)
        q_pair, k_pair, v_pair = queries[:, cols], keys[:, cols], values_in[:, cols]
        results = []
        for head in range(2):
            q_head = jnp.where((lane < HDIM) == (head == 0), q_pair, jnp.zeros_like(q_pair))
            scores = lax.dot_general(
                q_head, k_pair, (((1,), (1,)), ((), ())), preferred_element_type=F32
            )
            if interleaved:
                scores = jnp.where(same, scores, -jnp.inf)
            top = jnp.max(scores, axis=-1, keepdims=True)
            weights = jnp.exp(scores - top)
            denom = jnp.sum(weights, axis=-1, keepdims=True)
            results.append(dot(weights.astype(BF16), v_pair) / denom)
        contexts.append(jnp.where(lane < HDIM, results[0], results[1]).astype(BF16))
    return jnp.concatenate(contexts, axis=1)


def start_norm(tokens, gain_ref, normed_ref, total_ref):
    values = tokens.astype(F32)
    scale = lax.rsqrt(jnp.mean(values * values, axis=-1, keepdims=True) + 1e-06)
    normed_ref[...] = (values * scale * gain_ref[...]).astype(BF16)
    total_ref[...] = values


def add_heads(core_ref, normed_ref, mine_ref, theirs_ref, total_ref, interleaved):
    core = core_ref[0]
    half = normed_ref.shape[1] // 2
    at_mine = pl.multiple_of(core * half, half)
    at_theirs = pl.multiple_of(half - core * half, half)
    x_mine = normed_ref[:, pl.ds(at_mine, half)]
    x_theirs = normed_ref[:, pl.ds(at_theirs, half)]

    def project(member):
        w_mine = jnp.concatenate([mine_ref[0, member], mine_ref[1, member]], axis=1)
        w_theirs = jnp.concatenate([theirs_ref[0, member], theirs_ref[1, member]], axis=1)
        return dot(x_mine, w_mine) + dot(x_theirs, w_theirs)

    queries = (project(0) * HDIM ** (-0.5)).astype(BF16)
    context = attend(queries, project(1).astype(BF16), project(2).astype(BF16), interleaved)
    for ref, start in ((mine_ref, at_mine), (theirs_ref, at_theirs)):
        w_out = row_blocks((ref[0, 3], ref[1, 3]), 0, 128, 4)
        total_ref[:, pl.ds(start, half)] += dot(context, w_out)


def near_kernel(
    core_ref, x_ref, gain_ref, mine_ref, theirs_ref, *rest, interleaved
):
    total_ref, normed_ref = rest[-2:]

    @pl.when(pl.program_id(0) == 0)
    def _():
        unpack = unpack_tokens if interleaved else unpack_frame
        start_norm(unpack(x_ref[...]), gain_ref, normed_ref, total_ref)

    add_heads(core_ref, normed_ref, mine_ref, theirs_ref, total_ref, interleaved)


def far_kernel(
    core_ref, before_ref, normed_ref, mine_ref, theirs_ref, o_ref, total_ref, *, interleaved
):
    step = pl.program_id(0)

    @pl.when(step == 0)
    def _():
        total_ref[...] = before_ref[...]

    add_heads(core_ref, normed_ref, mine_ref, theirs_ref, total_ref, interleaved)

    @pl.when(step == pl.num_programs(0) - 1)
    def _():
        after = total_ref[...].astype(BF16)
        o_ref[...] = after if interleaved else pack_tokens(after)


def unpack_frame(arrived):
    senders, packed, lanes = arrived.shape
    tokens = packed // 8
    blocks = []
    for block in range(8):
        part = arrived[:, block * tokens : (block + 1) * tokens, :]
        blocks.append(part.reshape(senders * tokens, lanes))
    return jnp.concatenate(blocks, axis=1)


def moves(rows, source_of):
    row = lax.broadcasted_iota(jnp.int32, (rows, rows), 0)
    col = lax.broadcasted_iota(jnp.int32, (rows, rows), 1)
    return (source_of(row) == col).astype(F32).astype(BF16)


def pack_tokens(tokens):
    rows, width = tokens.shape
    blocks = width // 128
    by_dest = moves(rows, lambda i: (i // 2 % 8) * 32 + (i // 16) * 2 + i % 2)
    ordered = dot(by_dest, tokens).astype(BF16)
    mix = moves(rows, lambda i: (i // 2 % 8) * 32 + (i // 16) * 2 + i % 2)
    chunks = []
    depth = rows // blocks
    for part in range(blocks):
        piece = ordered[part * depth : (part + 1) * depth]
        stacked = [piece[:, k * 128 : (k + 1) * 128] for k in range(blocks)]
        mixed = dot(mix, jnp.concatenate(stacked, axis=0)).astype(BF16)
        chunks.append(mixed.reshape(rows // 16, 16, 128))
    return jnp.concatenate(chunks, axis=0)


def unpack_tokens(chunks):
    count, deep, lanes = chunks.shape
    rows = count * 2
    blocks = deep // 2
    mix = moves(rows, lambda i: (i // 2 % 16) * 16 + (i // 32) * 2 + i % 2)
    pieces = []
    for part in range(blocks):
        piece = chunks[part * 16 : (part + 1) * 16].reshape(rows, lanes)
        mixed = dot(mix, piece).astype(BF16)
        depth = rows // blocks
        columns = [mixed[k * depth : (k + 1) * depth] for k in range(blocks)]
        pieces.append(jnp.concatenate(columns, axis=1))
    return jnp.concatenate(pieces, axis=0)


ATTENTION_COST = pl.CostEstimate(
    flops=10 * 256 * 2**20, bytes_accessed=10 * 2**20, transcendentals=2**20
)
MLP_COST = pl.CostEstimate(
    flops=16 * 256 * 2**20, bytes_accessed=18 * 2**20, transcendentals=2**20
)
SPACE_COST = pl.CostEstimate(
    flops=5 * 256 * 2**20, bytes_accessed=6 * 2**20, transcendentals=2**19
)
SPACE_PARAMS = pltpu.CompilerParams(vmem_limit_bytes=16 * 2**20)
KERNEL_PARAMS = pltpu.CompilerParams(vmem_limit_bytes=58 * 2**20)


def near_block(core, tokens, gain, mine, theirs, interleaved, after=()):
    width = gain.shape[0]
    shape = tokens.shape if interleaved else (8, tokens.shape[1] // 2, 128)
    rows = shape[0] * shape[1] * shape[2] // width
    whole = (4, 4, width // 2, 128)
    weight_spec = pl.BlockSpec((2,) + whole[1:], lambda s: (s, 0, 0, 0))
    token_spec = pl.BlockSpec((rows, width), lambda s: (0, 0))
    return pl.pallas_call(
        functools.partial(near_kernel, interleaved=interleaved),
        out_shape=(
            jax.ShapeDtypeStruct((rows, width), F32),
            jax.ShapeDtypeStruct((rows, width), BF16),
        ),
        grid=(2,),
        in_specs=[
            pl.BlockSpec(memory_space=pltpu.SMEM),
            pl.BlockSpec(shape, lambda s: (0, 0, 0)),
            pl.BlockSpec((1, width), lambda s: (0, 0)),
            weight_spec,
            weight_spec,
        ]
        + [pl.BlockSpec(memory_space=pl.ANY)] * len(after),
        out_specs=(token_spec, token_spec),
        compiler_params=SPACE_PARAMS,
        cost_estimate=SPACE_COST,
    )(core, tokens, gain.reshape(1, width), mine.reshape(whole), theirs.reshape(whole), *after)


def far_block(core, total, normed, mine, theirs, interleaved):
    rows, width = total.shape
    whole = (4, 4, width // 2, 128)
    weight_spec = pl.BlockSpec((2,) + whole[1:], lambda s: (s, 0, 0, 0))
    token_spec = pl.BlockSpec((rows, width), lambda s: (0, 0))
    shape = (rows, width) if interleaved else (rows // 2, 2 * width // 128, 128)
    return pl.pallas_call(
        functools.partial(far_kernel, interleaved=interleaved),
        out_shape=jax.ShapeDtypeStruct(shape, BF16),
        grid=(2,),
        in_specs=[
            pl.BlockSpec(memory_space=pltpu.SMEM),
            token_spec,
            token_spec,
            weight_spec,
            weight_spec,
        ],
        out_specs=pl.BlockSpec(shape, lambda s: (0,) * len(shape)),
        scratch_shapes=[pltpu.VMEM((rows, width), F32)],
        compiler_params=SPACE_PARAMS,
        cost_estimate=SPACE_COST,
    )(core, total, normed, mine.reshape(whole), theirs.reshape(whole))


def gelu(inner):
    return (0.5 * inner * (1.0 + lax.erf(inner * 2.0 ** (-0.5)))).astype(BF16)


def row_blocks(pair, start, depth, count):
    blocks = []
    for block in range(count):
        rows = slice(start + block * depth, start + (block + 1) * depth)
        blocks.append(jnp.concatenate([part[rows] for part in pair], axis=0))
    return jnp.concatenate(blocks, axis=1)


def hidden_kernel(x_ref, gain_ref, in_ref, o_ref, normed_ref):
    ranks, shard_count, packed, lanes = in_ref.shape
    width = x_ref.shape[1]
    depth = width // ranks

    @pl.when(pl.program_id(0) == 0)
    def _():
        values = x_ref[...].astype(F32)
        scale = lax.rsqrt(jnp.mean(values * values, axis=-1, keepdims=True) + 1e-06)
        normed_ref[...] = (values * scale * gain_ref[...]).astype(BF16)

    columns = []
    for shard in range(shard_count):
        for block in range(packed // depth):
            part = in_ref[:, shard, block * depth : (block + 1) * depth, :]
            columns.append(part.reshape(width, lanes))
    o_ref[...] = gelu(dot(normed_ref[...], jnp.concatenate(columns, axis=1)))


def hidden_block(tokens, gain, w_in):
    rows, width = tokens.shape
    ranks, shard_count, packed, lanes = w_in.shape
    units = packed * ranks * lanes // width
    return pl.pallas_call(
        hidden_kernel,
        out_shape=jax.ShapeDtypeStruct((rows, shard_count * units), BF16),
        grid=(shard_count // 2,),
        in_specs=[
            pl.BlockSpec((rows, width), lambda s: (0, 0)),
            pl.BlockSpec((1, width), lambda s: (0, 0)),
            pl.BlockSpec((ranks, 2, packed, lanes), lambda s: (0, s, 0, 0)),
        ],
        out_specs=pl.BlockSpec((rows, 2 * units), lambda s: (0, s)),
        scratch_shapes=[pltpu.VMEM((rows, width), BF16)],
        compiler_params=KERNEL_PARAMS,
        cost_estimate=MLP_COST,
    )(tokens, gain.reshape(1, width), w_in)


def mlp_kernel(x_ref, head_ref, hidden_ref, out_ref, o_ref, total_ref):
    step = pl.program_id(0)
    ranks, shard_count, packed, lanes = out_ref.shape
    width = x_ref.shape[1]
    units = hidden_ref.shape[1] // shard_count

    @pl.when(step == 0)
    def _():
        total_ref[...] = x_ref[...].astype(F32)

    depth = units // ranks
    blocks = []
    for block in range(width // lanes):
        shards_of = []
        for shard in range(shard_count):
            part = out_ref[:, shard, block * depth : (block + 1) * depth, :]
            shards_of.append(part.reshape(units, lanes))
        blocks.append(jnp.concatenate(shards_of, axis=0))
    total_ref[...] += dot(hidden_ref[...], jnp.concatenate(blocks, axis=1))

    @pl.when(step == pl.num_programs(0) - 1)
    def _():
        features = total_ref[...].astype(BF16)
        dests = o_ref.shape[0]
        rows = features.shape[0] // dests
        for block in range(width // lanes):
            part = features[:, block * lanes : (block + 1) * lanes]
            o_ref[:, block * rows : (block + 1) * rows, :] = part.reshape(dests, rows, lanes)
        token_score = jnp.sum(features.astype(F32) * head_ref[...], axis=-1, keepdims=True)
        rest = jnp.zeros((rows, lanes), F32) + jnp.sum(jnp.exp(token_score))
        row = lax.broadcasted_iota(jnp.int32, (rows, lanes), 0)
        terms = jnp.zeros((rows, lanes), F32)
        for term in range(3):
            rounded = rest.astype(BF16).astype(F32)
            terms = jnp.where(row == term, rounded, terms)
            rest = rest - rounded
        last = rows * (width // lanes)
        for dest in range(dests):
            o_ref[dest, last:, :] = terms.astype(BF16)


def unpack_kernel(chunks_ref, o_ref):
    senders, rows, lanes = chunks_ref.shape
    per_block = rows // 9
    blocks = []
    for block in range(8):
        part = chunks_ref[:, block * per_block : (block + 1) * per_block, :]
        blocks.append(part.reshape(senders * per_block, lanes))
    order = moves(
        senders * per_block,
        lambda i: (i // 2 % senders) * per_block + (i // (2 * senders)) * 2 + i % 2,
    )
    o_ref[...] = dot(order, jnp.concatenate(blocks, axis=1)).astype(BF16)


def unpack_features(chunks, width):
    senders, rows, lanes = chunks.shape
    return pl.pallas_call(
        unpack_kernel,
        out_shape=jax.ShapeDtypeStruct((senders * rows // 9, width), BF16),
        compiler_params=pltpu.CompilerParams(vmem_limit_bytes=16 * 2**20),
    )(chunks)


def mlp_block(tokens, hidden, score_head, w_out):
    rows, width = tokens.shape
    ranks, shard_count, packed, lanes = w_out.shape
    shape = (ranks, rows // ranks * (width // lanes + 1), lanes)
    return pl.pallas_call(
        mlp_kernel,
        out_shape=jax.ShapeDtypeStruct(shape, BF16),
        grid=(shard_count // 2,),
        in_specs=[
            pl.BlockSpec((rows, width), lambda s: (0, 0)),
            pl.BlockSpec((1, width), lambda s: (0, 0)),
            pl.BlockSpec((rows, 2 * hidden.shape[1] // shard_count), lambda s: (0, s)),
            pl.BlockSpec((ranks, 2, packed, lanes), lambda s: (0, s, 0, 0)),
        ],
        out_specs=pl.BlockSpec(shape, lambda s: (0, 0, 0)),
        scratch_shapes=[pltpu.VMEM((rows, width), F32)],
        compiler_params=KERNEL_PARAMS,
        cost_estimate=MLP_COST,
    )(tokens, score_head.reshape(1, width), hidden, w_out)


def pack_attention_kernel(core_ref, qkv_ref, out_ref, packed_ref):
    depth = qkv_ref.shape[1]
    for member in range(3):
        packed_ref[member * depth : (member + 1) * depth, :] = qkv_ref[member]
    for block in range(depth // 128):
        start = 3 * depth + block * 128
        packed_ref[start : start + 128, :] = out_ref[:, block * 128 : (block + 1) * 128]


def pack_attention(core, qkv, out):
    members, width, local = qkv.shape
    half = width // 2
    return pl.pallas_call(
        pack_attention_kernel,
        out_shape=jax.ShapeDtypeStruct((4 * half, local), BF16),
        grid_spec=pltpu.PrefetchScalarGridSpec(
            num_scalar_prefetch=1,
            grid=(1,),
            in_specs=[
                pl.BlockSpec((members, half, local), lambda s, core_ref: (0, core_ref[0], 0)),
                pl.BlockSpec((local, half), lambda s, core_ref: (0, core_ref[0])),
            ],
            out_specs=pl.BlockSpec((4 * half, local), lambda s, core_ref: (0, 0)),
        ),
    )(core, qkv, out)


def pack_slice_kernel(rank_ref, in_ref, packed_ref):
    depth = in_ref.shape[0]
    for block in range(in_ref.shape[1] // 128):
        rows = slice(block * depth, (block + 1) * depth)
        for dest in range(packed_ref.shape[0]):
            packed_ref[dest, rows, :] = in_ref[:, block * 128 : (block + 1) * 128]


def pack_slice(rank, w_in, ranks, copies):
    width, units = w_in.shape
    depth = width // ranks
    shape = (copies, depth * units // 128, 128)
    return pl.pallas_call(
        pack_slice_kernel,
        out_shape=jax.ShapeDtypeStruct(shape, BF16),
        grid_spec=pltpu.PrefetchScalarGridSpec(
            num_scalar_prefetch=1,
            grid=(1,),
            in_specs=[pl.BlockSpec((depth, units), lambda s, rank_ref: (rank_ref[0], 0))],
            out_specs=pl.BlockSpec(shape, lambda s, rank_ref: (0, 0, 0)),
        ),
    )(rank, w_in)


def pack_send_kernel(rank_ref, video_ref, out_ref, packed_ref):
    tokens = video_ref.shape[1]
    first = packed_ref.shape[1] // 2
    depth = out_ref.shape[0]
    for block in range(video_ref.shape[2] // 128):
        columns = slice(block * 128, (block + 1) * 128)
        packed_ref[:, block * tokens : (block + 1) * tokens, :] = video_ref[:, :, columns]
        start = first + block * depth
        for dest in range(packed_ref.shape[0]):
            packed_ref[dest, start : start + depth, :] = out_ref[:, columns]


def pack_send(rank, video, w_out, ranks):
    units, width = w_out.shape
    depth = units // ranks
    frames, tokens, _ = video.shape
    shape = (frames, (tokens + depth) * width // 128, 128)
    return pl.pallas_call(
        pack_send_kernel,
        out_shape=jax.ShapeDtypeStruct(shape, BF16),
        grid_spec=pltpu.PrefetchScalarGridSpec(
            num_scalar_prefetch=1,
            grid=(1,),
            in_specs=[
                pl.BlockSpec((frames, tokens, width), lambda s, rank_ref: (0, 0, 0)),
                pl.BlockSpec((depth, width), lambda s, rank_ref: (rank_ref[0], 0)),
            ],
            out_specs=pl.BlockSpec(shape, lambda s, rank_ref: (0, 0, 0)),
        ),
    )(rank, video, w_out)


def shards(
    video,
    gain_space,
    qkv_space,
    out_space,
    gain_time,
    qkv_time,
    out_time,
    gain_mlp,
    w_in,
    w_out,
    score_head,
):
    frames, local_patches, width = video.shape
    patch_count = NX * 2
    clip_ranks = NZ * NCORE
    rows = frames * local_patches
    pairs = local_patches // clip_ranks
    frame_index = lax.axis_index("frame")
    core = frame_index % NCORE
    rank = frame_index % clip_ranks
    core_scalar = core.astype(jnp.int32).reshape(1)
    frame_groups = [[c * clip_ranks + i for i in range(clip_ranks)] for c in range(CLIPS)]
    clip_groups = [[c * 128 + i for i in range(128)] for c in range(CLIPS)]
    rank_groups = [
        [(c * clip_ranks + r) * patch_count + p for c in range(CLIPS) for p in range(patch_count)]
        for r in range(clip_ranks)
    ]

    space_own = pack_attention(core_scalar, qkv_space, out_space)
    space_own, video, rank_scalar = barrier(space_own, video, rank.astype(jnp.int32).reshape(1))
    space_left, space_right = first_phase_x(space_own)
    space_other = first_phase_y(space_own)
    def over_frame(slices):
        return lax.all_gather(slices, "frame", axis=0, axis_index_groups=frame_groups)

    in_slices = lax.all_to_all(
        pack_slice(rank_scalar, w_in, clip_ranks, patch_count), "patch", 0, 0, tiled=True
    )
    packed = pack_send(rank_scalar, video, w_out, clip_ranks)
    time_own = pack_attention(core_scalar, qkv_time, out_time)
    space_left, space_right, in_slices, packed, *space_other = barrier(
        space_left, space_right, in_slices, packed, *space_other
    )
    gathered_in = over_frame(in_slices)
    arrived = lax.all_to_all(packed, "patch", 0, 0, tiled=True)
    second = second_phase(space_left, space_right)
    (
        space_far_lo, space_far_hi, space_other_left, space_other_right, space_own, time_own,
        arrived,
    ) = barrier(*second, space_own, time_own, arrived)
    gathered_out = over_frame(arrived[:, arrived.shape[1] // 2 :])
    space_other_far = third_phase(space_far_lo, space_far_hi)
    time_left, time_right = first_phase_x(time_own)
    space_near = four(space_own, space_left, space_right, *space_other)
    space_near_other = swap(space_near)
    total, normed = near_block(
        core_scalar,
        arrived,
        gain_space,
        space_near,
        space_near_other,
        False,
    )
    space_far = four(
        space_other_left,
        space_other_right,
        space_far_lo,
        space_far_hi,
        *space_other_far,
        after=(total, time_left, time_right),
    )
    space_far_other = swap(space_far)
    time_other = shift(time_own, dy=1)
    after_space = far_block(core_scalar, total, normed, space_far, space_far_other, False)

    time_far, time_other_left = shift(time_left, dx=1), shift(time_left, dy=1)
    time_other_right = shift(time_right, dy=-1)
    time_other_far = shift(time_own, dx=2, dy=-1)
    by_patch = lax.all_to_all(after_space, AXES, 0, 0, tiled=True, axis_index_groups=clip_groups)
    time_near = four(time_own, time_left, time_right, time_other, after=(after_space,))
    time_near_other = swap(time_near)
    time_far = four(
        time_other_far, time_far, time_other_left, time_other_right, after=(by_patch,)
    )
    time_far_other = swap(time_far)
    total, normed = near_block(
        core_scalar, by_patch, gain_time, time_near, time_near_other, True
    )
    after_time = far_block(core_scalar, total, normed, time_far, time_far_other, True)
    hidden = hidden_block(after_time, gain_mlp, gathered_in)
    chunks = mlp_block(after_time, hidden, score_head, gathered_out)
    at_home = lax.all_to_all(
        chunks, "frame", 0, 0, tiled=True, axis_index_groups=frame_groups
    )
    last = at_home.shape[1] // 9 * 8
    part_sum = jnp.sum(at_home[:, last:, 0].astype(F32))
    sums = lax.all_to_all(
        jnp.broadcast_to(part_sum, (16, 8, 128)),
        AXES,
        0,
        0,
        tiled=True,
        axis_index_groups=rank_groups,
    )
    features = unpack_features(at_home, width).reshape(frames, local_patches, width)
    per_clip = jnp.sum(sums[:, 0, 0].reshape(CLIPS, patch_count), axis=1)
    score = jnp.log(per_clip / (frames * clip_ranks * local_patches * patch_count))
    return (features, score)


def solution(mesh):
    placed = (
        P("frame", "patch", None),
        P(),
        P(None, None, "patch"),
        P("patch", None),
        P(),
        P(None, None, "patch"),
        P("patch", None),
        P(),
        P(None, "patch"),
        P("patch", None),
        P(),
    )
    return jax.shard_map(
        shards,
        mesh=mesh,
        in_specs=placed,
        out_specs=(P("frame", "patch", None), P()),
        check_vma=False,
    )
```

```python
import functools

import jax
import jax.numpy as jnp
from jax import lax
from jax.experimental import pallas as pl
from jax.experimental.pallas import tpu as pltpu
from jax.sharding import PartitionSpec as P

HDIM = 64
CLIPS = 2
NX, NY, NZ, NCORE = 4, 4, 8, 2
AXES = ("frame", "patch")
BF16 = jnp.bfloat16
F32 = jnp.float32


def place(flat):
    frame, patch = divmod(flat, NX * 2)
    y_hi, rest = divmod(frame, NZ * NCORE)
    z, core = divmod(rest, NCORE)
    y_lo, x = divmod(patch, NX)
    return x, y_hi * 2 + y_lo, z, core


def flat_of(x, y, z, core):
    y_hi, y_lo = divmod(y % NY, 2)
    return ((y_hi * NZ + z % NZ) * NCORE + core % NCORE) * (NX * 2) + y_lo * NX + x % NX


def shift(value, dx=0, dy=0, dz=0, dc=0):
    pairs = []
    for flat in range(NX * NY * NZ * NCORE):
        x, y, z, core = place(flat)
        pairs.append((flat, flat_of(x + dx, y + dy, z + dz, core + dc)))
    return lax.ppermute(value, AXES, pairs)


def dot(left, right):
    return jnp.dot(left, right, preferred_element_type=F32)


def barrier(*values):
    return lax.optimization_barrier(values)


def first_phase_x(own):
    return shift(own, dx=1), shift(own, dx=-1)


def first_phase_y(own):
    cut = own.shape[0] // 2
    return shift(own[:cut], dy=1), shift(own[cut:], dy=-1)


def second_phase(left, right):
    cut = left.shape[0] // 2
    far_lo, far_hi = shift(left[:cut], dx=1), shift(right[cut:], dx=-1)
    return far_lo, far_hi, shift(left, dy=1), shift(right, dy=-1)


def third_phase(far_lo, far_hi):
    return shift(far_lo, dy=1), shift(far_hi, dy=-1)


def join_kernel(count, *refs):
    joined_ref, sems = refs[-2:]
    copies = []
    start = 0
    for at, part in enumerate(refs[:count]):
        rows = pl.ds(start, part.shape[0])
        copies.append(pltpu.make_async_copy(part, joined_ref.at[rows], sems.at[at]))
        start += part.shape[0]
    for copy in copies:
        copy.start()
    for copy in copies:
        copy.wait()


def four(*parts, after=()):
    rows = sum(part.shape[0] for part in parts)
    return pl.pallas_call(
        functools.partial(join_kernel, len(parts)),
        out_shape=jax.ShapeDtypeStruct((rows,) + parts[0].shape[1:], BF16),
        in_specs=[pl.BlockSpec(memory_space=pl.ANY)] * (len(parts) + len(after)),
        out_specs=pl.BlockSpec(memory_space=pltpu.VMEM),
        scratch_shapes=[pltpu.SemaphoreType.DMA((len(parts),))],
        compiler_params=pltpu.CompilerParams(vmem_limit_bytes=16 * 2**20),
    )(*parts, *after)


def swap(part):
    return shift(part, dc=1)


def attend(queries, keys, values_in, interleaved):
    tokens = queries.shape[0]
    lane = lax.broadcasted_iota(jnp.int32, (tokens, 2 * HDIM), 1)
    if interleaved:
        row = lax.broadcasted_iota(jnp.int32, (tokens, tokens), 0)
        col = lax.broadcasted_iota(jnp.int32, (tokens, tokens), 1)
        same = (row & 1) == (col & 1)
    contexts = []
    for pair in range(2):
        cols = slice(pair * 2 * HDIM, (pair + 1) * 2 * HDIM)
        q_pair, k_pair, v_pair = queries[:, cols], keys[:, cols], values_in[:, cols]
        results = []
        for head in range(2):
            q_head = jnp.where((lane < HDIM) == (head == 0), q_pair, jnp.zeros_like(q_pair))
            scores = lax.dot_general(
                q_head, k_pair, (((1,), (1,)), ((), ())), preferred_element_type=F32
            )
            if interleaved:
                scores = jnp.where(same, scores, -jnp.inf)
            top = jnp.max(scores, axis=-1, keepdims=True)
            weights = jnp.exp(scores - top)
            denom = jnp.sum(weights, axis=-1, keepdims=True)
            results.append(dot(weights.astype(BF16), v_pair) / denom)
        contexts.append(jnp.where(lane < HDIM, results[0], results[1]).astype(BF16))
    return jnp.concatenate(contexts, axis=1)


def start_norm(tokens, gain_ref, normed_ref, total_ref):
    values = tokens.astype(F32)
    scale = lax.rsqrt(jnp.mean(values * values, axis=-1, keepdims=True) + 1e-06)
    normed_ref[...] = (values * scale * gain_ref[...]).astype(BF16)
    total_ref[...] = values


def add_heads(core_ref, normed_ref, mine_ref, theirs_ref, total_ref, interleaved):
    core = core_ref[0]
    half = normed_ref.shape[1] // 2
    at_mine = pl.multiple_of(core * half, half)
    at_theirs = pl.multiple_of(half - core * half, half)
    x_mine = normed_ref[:, pl.ds(at_mine, half)]
    x_theirs = normed_ref[:, pl.ds(at_theirs, half)]

    def project(member):
        w_mine = jnp.concatenate([mine_ref[0, member], mine_ref[1, member]], axis=1)
        w_theirs = jnp.concatenate([theirs_ref[0, member], theirs_ref[1, member]], axis=1)
        return dot(x_mine, w_mine) + dot(x_theirs, w_theirs)

    queries = (project(0) * HDIM ** (-0.5)).astype(BF16)
    context = attend(queries, project(1).astype(BF16), project(2).astype(BF16), interleaved)
    for ref, start in ((mine_ref, at_mine), (theirs_ref, at_theirs)):
        w_out = row_blocks((ref[0, 3], ref[1, 3]), 0, 128, 4)
        total_ref[:, pl.ds(start, half)] += dot(context, w_out)


def near_kernel(
    core_ref, x_ref, gain_ref, mine_ref, theirs_ref, *rest, interleaved
):
    total_ref, normed_ref = rest[-2:]

    @pl.when(pl.program_id(0) == 0)
    def _():
        unpack = unpack_tokens if interleaved else unpack_frame
        start_norm(unpack(x_ref[...]), gain_ref, normed_ref, total_ref)

    add_heads(core_ref, normed_ref, mine_ref, theirs_ref, total_ref, interleaved)


def far_kernel(
    core_ref, before_ref, normed_ref, mine_ref, theirs_ref, o_ref, total_ref, *, interleaved
):
    step = pl.program_id(0)

    @pl.when(step == 0)
    def _():
        total_ref[...] = before_ref[...]

    add_heads(core_ref, normed_ref, mine_ref, theirs_ref, total_ref, interleaved)

    @pl.when(step == pl.num_programs(0) - 1)
    def _():
        after = total_ref[...].astype(BF16)
        o_ref[...] = after if interleaved else pack_tokens(after)


def unpack_frame(arrived):
    senders, packed, lanes = arrived.shape
    tokens = packed // 8
    blocks = []
    for block in range(8):
        part = arrived[:, block * tokens : (block + 1) * tokens, :]
        blocks.append(part.reshape(senders * tokens, lanes))
    return jnp.concatenate(blocks, axis=1)


def moves(rows, source_of):
    row = lax.broadcasted_iota(jnp.int32, (rows, rows), 0)
    col = lax.broadcasted_iota(jnp.int32, (rows, rows), 1)
    return (source_of(row) == col).astype(F32).astype(BF16)


def pack_tokens(tokens):
    rows, width = tokens.shape
    blocks = width // 128
    by_dest = moves(rows, lambda i: (i // 2 % 8) * 32 + (i // 16) * 2 + i % 2)
    ordered = dot(by_dest, tokens).astype(BF16)
    mix = moves(rows, lambda i: (i // 2 % 8) * 32 + (i // 16) * 2 + i % 2)
    chunks = []
    depth = rows // blocks
    for part in range(blocks):
        piece = ordered[part * depth : (part + 1) * depth]
        stacked = [piece[:, k * 128 : (k + 1) * 128] for k in range(blocks)]
        mixed = dot(mix, jnp.concatenate(stacked, axis=0)).astype(BF16)
        chunks.append(mixed.reshape(rows // 16, 16, 128))
    return jnp.concatenate(chunks, axis=0)


def unpack_tokens(chunks):
    count, deep, lanes = chunks.shape
    rows = count * 2
    blocks = deep // 2
    mix = moves(rows, lambda i: (i // 2 % 16) * 16 + (i // 32) * 2 + i % 2)
    pieces = []
    for part in range(blocks):
        piece = chunks[part * 16 : (part + 1) * 16].reshape(rows, lanes)
        mixed = dot(mix, piece).astype(BF16)
        depth = rows // blocks
        columns = [mixed[k * depth : (k + 1) * depth] for k in range(blocks)]
        pieces.append(jnp.concatenate(columns, axis=1))
    return jnp.concatenate(pieces, axis=0)


ATTENTION_COST = pl.CostEstimate(
    flops=10 * 256 * 2**20, bytes_accessed=10 * 2**20, transcendentals=2**20
)
MLP_COST = pl.CostEstimate(
    flops=16 * 256 * 2**20, bytes_accessed=18 * 2**20, transcendentals=2**20
)
SPACE_COST = pl.CostEstimate(
    flops=5 * 256 * 2**20, bytes_accessed=6 * 2**20, transcendentals=2**19
)
SPACE_PARAMS = pltpu.CompilerParams(vmem_limit_bytes=16 * 2**20)
KERNEL_PARAMS = pltpu.CompilerParams(vmem_limit_bytes=58 * 2**20)


def near_block(core, tokens, gain, mine, theirs, interleaved, after=()):
    width = gain.shape[0]
    shape = tokens.shape if interleaved else (8, tokens.shape[1] // 2, 128)
    rows = shape[0] * shape[1] * shape[2] // width
    whole = (4, 4, width // 2, 128)
    weight_spec = pl.BlockSpec((2,) + whole[1:], lambda s: (s, 0, 0, 0))
    token_spec = pl.BlockSpec((rows, width), lambda s: (0, 0))
    return pl.pallas_call(
        functools.partial(near_kernel, interleaved=interleaved),
        out_shape=(
            jax.ShapeDtypeStruct((rows, width), F32),
            jax.ShapeDtypeStruct((rows, width), BF16),
        ),
        grid=(2,),
        in_specs=[
            pl.BlockSpec(memory_space=pltpu.SMEM),
            pl.BlockSpec(shape, lambda s: (0, 0, 0)),
            pl.BlockSpec((1, width), lambda s: (0, 0)),
            weight_spec,
            weight_spec,
        ]
        + [pl.BlockSpec(memory_space=pl.ANY)] * len(after),
        out_specs=(token_spec, token_spec),
        compiler_params=SPACE_PARAMS,
        cost_estimate=SPACE_COST,
    )(core, tokens, gain.reshape(1, width), mine.reshape(whole), theirs.reshape(whole), *after)


def far_block(core, total, normed, mine, theirs, interleaved):
    rows, width = total.shape
    whole = (4, 4, width // 2, 128)
    weight_spec = pl.BlockSpec((2,) + whole[1:], lambda s: (s, 0, 0, 0))
    token_spec = pl.BlockSpec((rows, width), lambda s: (0, 0))
    shape = (rows, width) if interleaved else (rows // 2, 2 * width // 128, 128)
    return pl.pallas_call(
        functools.partial(far_kernel, interleaved=interleaved),
        out_shape=jax.ShapeDtypeStruct(shape, BF16),
        grid=(2,),
        in_specs=[
            pl.BlockSpec(memory_space=pltpu.SMEM),
            token_spec,
            token_spec,
            weight_spec,
            weight_spec,
        ],
        out_specs=pl.BlockSpec(shape, lambda s: (0,) * len(shape)),
        scratch_shapes=[pltpu.VMEM((rows, width), F32)],
        compiler_params=SPACE_PARAMS,
        cost_estimate=SPACE_COST,
    )(core, total, normed, mine.reshape(whole), theirs.reshape(whole))


def gelu(inner):
    return (0.5 * inner * (1.0 + lax.erf(inner * 2.0 ** (-0.5)))).astype(BF16)


def row_blocks(pair, start, depth, count):
    blocks = []
    for block in range(count):
        rows = slice(start + block * depth, start + (block + 1) * depth)
        blocks.append(jnp.concatenate([part[rows] for part in pair], axis=0))
    return jnp.concatenate(blocks, axis=1)


def hidden_kernel(x_ref, gain_ref, in_ref, o_ref, normed_ref):
    ranks, shard_count, packed, lanes = in_ref.shape
    width = x_ref.shape[1]
    depth = width // ranks

    @pl.when(pl.program_id(0) == 0)
    def _():
        values = x_ref[...].astype(F32)
        scale = lax.rsqrt(jnp.mean(values * values, axis=-1, keepdims=True) + 1e-06)
        normed_ref[...] = (values * scale * gain_ref[...]).astype(BF16)

    columns = []
    for shard in range(shard_count):
        for block in range(packed // depth):
            part = in_ref[:, shard, block * depth : (block + 1) * depth, :]
            columns.append(part.reshape(width, lanes))
    o_ref[...] = gelu(dot(normed_ref[...], jnp.concatenate(columns, axis=1)))


def hidden_block(tokens, gain, w_in):
    rows, width = tokens.shape
    ranks, shard_count, packed, lanes = w_in.shape
    units = packed * ranks * lanes // width
    return pl.pallas_call(
        hidden_kernel,
        out_shape=jax.ShapeDtypeStruct((rows, shard_count * units), BF16),
        grid=(shard_count // 2,),
        in_specs=[
            pl.BlockSpec((rows, width), lambda s: (0, 0)),
            pl.BlockSpec((1, width), lambda s: (0, 0)),
            pl.BlockSpec((ranks, 2, packed, lanes), lambda s: (0, s, 0, 0)),
        ],
        out_specs=pl.BlockSpec((rows, 2 * units), lambda s: (0, s)),
        scratch_shapes=[pltpu.VMEM((rows, width), BF16)],
        compiler_params=KERNEL_PARAMS,
        cost_estimate=MLP_COST,
    )(tokens, gain.reshape(1, width), w_in)


def mlp_kernel(x_ref, head_ref, hidden_ref, out_ref, o_ref, total_ref):
    step = pl.program_id(0)
    ranks, shard_count, packed, lanes = out_ref.shape
    width = x_ref.shape[1]
    units = hidden_ref.shape[1] // shard_count

    @pl.when(step == 0)
    def _():
        total_ref[...] = x_ref[...].astype(F32)

    depth = units // ranks
    blocks = []
    for block in range(width // lanes):
        shards_of = []
        for shard in range(shard_count):
            part = out_ref[:, shard, block * depth : (block + 1) * depth, :]
            shards_of.append(part.reshape(units, lanes))
        blocks.append(jnp.concatenate(shards_of, axis=0))
    total_ref[...] += dot(hidden_ref[...], jnp.concatenate(blocks, axis=1))

    @pl.when(step == pl.num_programs(0) - 1)
    def _():
        features = total_ref[...].astype(BF16)
        dests = o_ref.shape[0]
        rows = features.shape[0] // dests
        for block in range(width // lanes):
            part = features[:, block * lanes : (block + 1) * lanes]
            o_ref[:, block * rows : (block + 1) * rows, :] = part.reshape(dests, rows, lanes)
        token_score = jnp.sum(features.astype(F32) * head_ref[...], axis=-1, keepdims=True)
        rest = jnp.zeros((rows, lanes), F32) + jnp.sum(jnp.exp(token_score))
        row = lax.broadcasted_iota(jnp.int32, (rows, lanes), 0)
        terms = jnp.zeros((rows, lanes), F32)
        for term in range(3):
            rounded = rest.astype(BF16).astype(F32)
            terms = jnp.where(row == term, rounded, terms)
            rest = rest - rounded
        last = rows * (width // lanes)
        for dest in range(dests):
            o_ref[dest, last:, :] = terms.astype(BF16)


def unpack_kernel(chunks_ref, o_ref):
    senders, rows, lanes = chunks_ref.shape
    per_block = rows // 9
    blocks = []
    for block in range(8):
        part = chunks_ref[:, block * per_block : (block + 1) * per_block, :]
        blocks.append(part.reshape(senders * per_block, lanes))
    order = moves(
        senders * per_block,
        lambda i: (i // 2 % senders) * per_block + (i // (2 * senders)) * 2 + i % 2,
    )
    o_ref[...] = dot(order, jnp.concatenate(blocks, axis=1)).astype(BF16)


def unpack_features(chunks, width):
    senders, rows, lanes = chunks.shape
    return pl.pallas_call(
        unpack_kernel,
        out_shape=jax.ShapeDtypeStruct((senders * rows // 9, width), BF16),
        compiler_params=pltpu.CompilerParams(vmem_limit_bytes=16 * 2**20),
    )(chunks)


def mlp_block(tokens, hidden, score_head, w_out):
    rows, width = tokens.shape
    ranks, shard_count, packed, lanes = w_out.shape
    shape = (ranks, rows // ranks * (width // lanes + 1), lanes)
    return pl.pallas_call(
        mlp_kernel,
        out_shape=jax.ShapeDtypeStruct(shape, BF16),
        grid=(shard_count // 2,),
        in_specs=[
            pl.BlockSpec((rows, width), lambda s: (0, 0)),
            pl.BlockSpec((1, width), lambda s: (0, 0)),
            pl.BlockSpec((rows, 2 * hidden.shape[1] // shard_count), lambda s: (0, s)),
            pl.BlockSpec((ranks, 2, packed, lanes), lambda s: (0, s, 0, 0)),
        ],
        out_specs=pl.BlockSpec(shape, lambda s: (0, 0, 0)),
        scratch_shapes=[pltpu.VMEM((rows, width), F32)],
        compiler_params=KERNEL_PARAMS,
        cost_estimate=MLP_COST,
    )(tokens, score_head.reshape(1, width), hidden, w_out)


def pack_attention_kernel(core_ref, qkv_ref, out_ref, packed_ref):
    depth = qkv_ref.shape[1]
    for member in range(3):
        packed_ref[member * depth : (member + 1) * depth, :] = qkv_ref[member]
    for block in range(depth // 128):
        start = 3 * depth + block * 128
        packed_ref[start : start + 128, :] = out_ref[:, block * 128 : (block + 1) * 128]


def pack_attention(core, qkv, out):
    members, width, local = qkv.shape
    half = width // 2
    return pl.pallas_call(
        pack_attention_kernel,
        out_shape=jax.ShapeDtypeStruct((4 * half, local), BF16),
        grid_spec=pltpu.PrefetchScalarGridSpec(
            num_scalar_prefetch=1,
            grid=(1,),
            in_specs=[
                pl.BlockSpec((members, half, local), lambda s, core_ref: (0, core_ref[0], 0)),
                pl.BlockSpec((local, half), lambda s, core_ref: (0, core_ref[0])),
            ],
            out_specs=pl.BlockSpec((4 * half, local), lambda s, core_ref: (0, 0)),
        ),
    )(core, qkv, out)


def pack_slice_kernel(rank_ref, in_ref, packed_ref):
    depth = in_ref.shape[0]
    for block in range(in_ref.shape[1] // 128):
        rows = slice(block * depth, (block + 1) * depth)
        for dest in range(packed_ref.shape[0]):
            packed_ref[dest, rows, :] = in_ref[:, block * 128 : (block + 1) * 128]


def pack_slice(rank, w_in, ranks, copies):
    width, units = w_in.shape
    depth = width // ranks
    shape = (copies, depth * units // 128, 128)
    return pl.pallas_call(
        pack_slice_kernel,
        out_shape=jax.ShapeDtypeStruct(shape, BF16),
        grid_spec=pltpu.PrefetchScalarGridSpec(
            num_scalar_prefetch=1,
            grid=(1,),
            in_specs=[pl.BlockSpec((depth, units), lambda s, rank_ref: (rank_ref[0], 0))],
            out_specs=pl.BlockSpec(shape, lambda s, rank_ref: (0, 0, 0)),
        ),
    )(rank, w_in)


def pack_send_kernel(rank_ref, video_ref, out_ref, packed_ref):
    tokens = video_ref.shape[1]
    first = packed_ref.shape[1] // 2
    depth = out_ref.shape[0]
    for block in range(video_ref.shape[2] // 128):
        columns = slice(block * 128, (block + 1) * 128)
        packed_ref[:, block * tokens : (block + 1) * tokens, :] = video_ref[:, :, columns]
        start = first + block * depth
        for dest in range(packed_ref.shape[0]):
            packed_ref[dest, start : start + depth, :] = out_ref[:, columns]


def pack_send(rank, video, w_out, ranks):
    units, width = w_out.shape
    depth = units // ranks
    frames, tokens, _ = video.shape
    shape = (frames, (tokens + depth) * width // 128, 128)
    return pl.pallas_call(
        pack_send_kernel,
        out_shape=jax.ShapeDtypeStruct(shape, BF16),
        grid_spec=pltpu.PrefetchScalarGridSpec(
            num_scalar_prefetch=1,
            grid=(1,),
            in_specs=[
                pl.BlockSpec((frames, tokens, width), lambda s, rank_ref: (0, 0, 0)),
                pl.BlockSpec((depth, width), lambda s, rank_ref: (rank_ref[0], 0)),
            ],
            out_specs=pl.BlockSpec(shape, lambda s, rank_ref: (0, 0, 0)),
        ),
    )(rank, video, w_out)


def shards(
    video,
    gain_space,
    qkv_space,
    out_space,
    gain_time,
    qkv_time,
    out_time,
    gain_mlp,
    w_in,
    w_out,
    score_head,
):
    frames, local_patches, width = video.shape
    patch_count = NX * 2
    clip_ranks = NZ * NCORE
    rows = frames * local_patches
    pairs = local_patches // clip_ranks
    frame_index = lax.axis_index("frame")
    core = frame_index % NCORE
    rank = frame_index % clip_ranks
    core_scalar = core.astype(jnp.int32).reshape(1)
    frame_groups = [[c * clip_ranks + i for i in range(clip_ranks)] for c in range(CLIPS)]
    clip_groups = [[c * 128 + i for i in range(128)] for c in range(CLIPS)]
    rank_groups = [
        [(c * clip_ranks + r) * patch_count + p for c in range(CLIPS) for p in range(patch_count)]
        for r in range(clip_ranks)
    ]

    space_own = pack_attention(core_scalar, qkv_space, out_space)
    space_own, video, rank_scalar = barrier(space_own, video, rank.astype(jnp.int32).reshape(1))
    space_left, space_right = first_phase_x(space_own)
    space_other = first_phase_y(space_own)
    def over_frame(slices):
        return lax.all_gather(slices, "frame", axis=0, axis_index_groups=frame_groups)

    in_slices = lax.all_to_all(
        pack_slice(rank_scalar, w_in, clip_ranks, patch_count), "patch", 0, 0, tiled=True
    )
    packed = pack_send(rank_scalar, video, w_out, clip_ranks)
    time_own = pack_attention(core_scalar, qkv_time, out_time)
    space_left, space_right, packed, *space_other = barrier(
        space_left, space_right, packed, *space_other
    )
    gathered_in = over_frame(in_slices)
    arrived = lax.all_to_all(packed, "patch", 0, 0, tiled=True)
    second = second_phase(space_left, space_right)
    (
        space_far_lo, space_far_hi, space_other_left, space_other_right, space_own, time_own,
        arrived,
    ) = barrier(*second, space_own, time_own, arrived)
    gathered_out = over_frame(arrived[:, arrived.shape[1] // 2 :])
    space_other_far = third_phase(space_far_lo, space_far_hi)
    time_left, time_right = first_phase_x(time_own)
    space_near = four(space_own, space_left, space_right, *space_other)
    space_near_other = swap(space_near)
    total, normed = near_block(
        core_scalar,
        arrived,
        gain_space,
        space_near,
        space_near_other,
        False,
    )
    space_far = four(
        space_other_left,
        space_other_right,
        space_far_lo,
        space_far_hi,
        *space_other_far,
        after=(total, time_left, time_right),
    )
    space_far_other = swap(space_far)
    time_other = shift(time_own, dy=1)
    after_space = far_block(core_scalar, total, normed, space_far, space_far_other, False)

    time_far, time_other_left = shift(time_left, dx=1), shift(time_left, dy=1)
    time_other_right = shift(time_right, dy=-1)
    time_other_far = shift(time_own, dx=2, dy=-1)
    by_patch = lax.all_to_all(after_space, AXES, 0, 0, tiled=True, axis_index_groups=clip_groups)
    time_near = four(time_own, time_left, time_right, time_other, after=(after_space,))
    time_near_other = swap(time_near)
    time_far = four(
        time_other_far, time_far, time_other_left, time_other_right, after=(time_near_other,)
    )
    time_far_other = swap(time_far)
    total, normed = near_block(
        core_scalar, by_patch, gain_time, time_near, time_near_other, True
    )
    after_time = far_block(core_scalar, total, normed, time_far, time_far_other, True)
    hidden = hidden_block(after_time, gain_mlp, gathered_in)
    chunks = mlp_block(after_time, hidden, score_head, gathered_out)
    at_home = lax.all_to_all(
        chunks, "frame", 0, 0, tiled=True, axis_index_groups=frame_groups
    )
    last = at_home.shape[1] // 9 * 8
    part_sum = jnp.sum(at_home[:, last:, 0].astype(F32))
    sums = lax.all_to_all(
        jnp.broadcast_to(part_sum, (16, 8, 128)),
        AXES,
        0,
        0,
        tiled=True,
        axis_index_groups=rank_groups,
    )
    features = unpack_features(at_home, width).reshape(frames, local_patches, width)
    per_clip = jnp.sum(sums[:, 0, 0].reshape(CLIPS, patch_count), axis=1)
    score = jnp.log(per_clip / (frames * clip_ranks * local_patches * patch_count))
    return (features, score)


def solution(mesh):
    placed = (
        P("frame", "patch", None),
        P(),
        P(None, None, "patch"),
        P("patch", None),
        P(),
        P(None, None, "patch"),
        P("patch", None),
        P(),
        P(None, "patch"),
        P("patch", None),
        P(),
    )
    return jax.shard_map(
        shards,
        mesh=mesh,
        in_specs=placed,
        out_specs=(P("frame", "patch", None), P()),
        check_vma=False,
    )
```
